128 devices in a mesh: section: 2 (over core), expert: 4 (over x), seq: 16 (over z, y).
Axes of the slice: x: 4, y: 4, z: 4, core: 2. Of those that a mesh axis runs over, the one named last changes fastest.
Arguments:
- entry_rows: bfloat16 [4, 32, 2048], P('section', 'expert'), may hold values from -6 to 6
- cache_entries: bfloat16 [2, 32, 2, 4096, 512], P('section', 'expert', None, 'seq'), may hold values from -250 to 250
- cache_lengths: int32 [4, 32], P(None, 'expert'), may hold values from 1 to 4096, as said below
- norm_gains: float32 [2, 2, 2048], P('section'), may hold values from 0.1 to 1.9
- expert_ids: int32 [2, 4, 32, 8], P('section', None, 'expert'), may hold values from 0 to 63, all different within a row; in each aligned block of 8 rows (0 to 7, 8 to 15, ..., all dimensions but the last counted through in order) at most 2 rows name the same one
- gate_weights: float32 [2, 4, 32, 8], P('section', None, 'expert'), may hold values from 0.1 to 1
- gate_weight: bfloat16 [2, 64, 768, 2048], P('section', ('expert', 'seq')), may hold values from -0.125 to 0.125
- up_weight: bfloat16 [2, 64, 768, 2048], P('section', ('expert', 'seq')), may hold values from -0.125 to 0.125
- down_weight: bfloat16 [2, 64, 768, 2048], P('section', ('expert', 'seq')), may hold values from -0.21875 to 0.21875
- codebook_ids: int32 [4, 32], P(None, 'expert'), may hold values from 0 to 1023
- codec_table: bfloat16 [1024, 2048], P(('section', 'seq')), may hold values from -6 to 6
- final_gain: float32 [2048], replicated, may hold values from 0.1 to 1.9
Outputs:
- codec_logits: float32 [4, 32, 1024], P(None, 'expert', ('section', 'seq'))
The draws below stay inside these ranges and needn't reach their ends.
Inputs may be any that keep to these rules, and one draw needn't show every extreme that they name: `expert_ids`: in each aligned block of 8 rows (one index of expert's rows of one layer and step) no expert is named by more than 2 rows, a bound that some block reaches. `cache_lengths`: at every step some row has seen all 4096 positions.
All inputs are finite; a program needn't handle non-finite values.
Results may differ from the reference program's by a relative error of at most 0.012.
The reference program's roundings to bfloat16 on the way count: a program that leaves them out, or rounds other values in their place, can miss the bound.
Values may be sent and summed in bfloat16 or wider, within the bound.
No kernel may reach another device: no remote copies, remote signals or barrier semaphores. Data moves between devices by JAX's collectives and lax.ppermute only.
A program may use at most 128 MiB of HBM per device.

```python
import math
import jax
import jax.numpy as jnp
import numpy as np
from jax import lax

D = 2048
HEAD_DIM = 128
KV_HEADS = 4
FF = 768
EXPERTS = 64
TOP = 8
LAYERS = 2
STEPS = 4
ROWS_DEV = 8
ROWS = 32
CTX = 4096
CAP = 2
CODES = 1024
N_EXPERT = 4


def draw_cache_entries(key, part):
    key = jax.random.fold_in(key, 11)
    draw_one = jax.random.fold_in(key, 0)
    kv_width = KV_HEADS * HEAD_DIM
    base_draw = jax.random.normal(draw_one, (LAYERS, ROWS, 2, CTX, kv_width), jnp.float32)
    return jnp.clip(base_draw, -6.0, 6.0).astype(jnp.bfloat16)


def draw_cache_lengths(key, part):
    key = jax.random.fold_in(key, 23)
    draw_one, draw_two = jax.random.split(key)
    lengths = jax.random.randint(draw_one, (STEPS, ROWS), 1, CTX + 1, jnp.int32)
    longest = jax.random.randint(draw_two, (STEPS, 1), 0, ROWS, jnp.int32)
    return jnp.where(jnp.arange(ROWS, dtype=jnp.int32)[None, :] == longest, CTX, lengths).astype(jnp.int32)


def with_ends(values, key, smallest, largest):
    longest = values.shape.index(max(values.shape))
    spots = []
    for shift in (0, 1):
        where = [jax.random.randint(jax.random.fold_in(key, axis), (), 0, length) for axis, length in enumerate(values.shape)]
        where[longest] = (where[longest] + shift) % values.shape[longest]
        spots.append(tuple(where))
    return values.at[spots[0]].set(smallest).at[spots[1]].set(largest)


def levels(stream_key, dims, pieces, low, largest):
    def one(axis_at, shards_of):
        draws = jax.random.uniform(jax.random.fold_in(jax.random.fold_in(stream_key, 6), axis_at), (shards_of,), jnp.float32, low / len(pieces), largest / len(pieces))
        return jnp.repeat(jnp.exp(draws), dims[axis_at] // shards_of).reshape((-1,) + (1,) * (len(dims) - axis_at - 1))

    level = one(*pieces[0])
    for cut in pieces[1:]:
        level = level * one(*cut)
    return level


def cumulative_ranks(number_of, slope):
    portions = [(1 << 20) // math.isqrt(rank ** slope) + 1 for rank in range(1, number_of + 1)]
    width = 1 + sum(portions) // (1 << 30)
    return np.cumsum(np.array([max(1, weight // width) for weight in portions]))


def ranked(key, shape, amount, slope):
    grid = cumulative_ranks(amount, slope)
    pick = jax.random.randint(jax.random.fold_in(key, 1), shape, 0, int(grid[amount - 1]))
    rank = jnp.searchsorted(jnp.asarray(grid, jnp.int32), pick, side="right")
    return jax.random.permutation(jax.random.fold_in(key, 2), amount)[rank].astype(jnp.int32)


def assign_block(own_key, own, number, rows, number_of, top, bound, lean):
    order = jax.random.permutation(own_key, number_of)
    packed, usual = load_shares(number_of, rows * top, bound, lean, True), load_shares(number_of, rows * top, bound, lean, False)
    places = jnp.arange(number_of)

    def named(tallies, offset_by):
        used = int((tallies > 0).sum())
        fixed = max(1, used // 4)
        passed = fixed + (places - fixed + offset_by * (used - fixed)) % max(1, number_of - fixed)
        return jnp.zeros((number_of,), jnp.int32).at[order[jnp.where(places < fixed, places, passed)]].set(jnp.asarray(tallies, jnp.int32))

    tallies = jnp.where(number % 4 == 0, named(packed, number // 4), named(usual, number - number // 4 - 1))
    mixed = jax.random.permutation(jax.random.fold_in(own, 3), number_of)
    donor, sink = mixed[0:number_of // 2 * 2:2], mixed[1:number_of // 2 * 2:2]
    margin = jnp.minimum(tallies[donor] - 1, bound - tallies[sink]) // 2
    margin = jnp.where((donor == order[0]) | (sink == order[0]) | (tallies[sink] == 0), 0, jnp.maximum(margin, 0))
    passed = jax.random.randint(jax.random.fold_in(own, 4), (number_of // 2,), 0, 1 << 20) % (margin + 1)
    tallies = tallies.at[donor].add(-passed).at[sink].add(passed)
    members = jnp.searchsorted(jnp.cumsum(tallies), jnp.arange(rows * top), side="right").astype(jnp.int32)
    table = members.reshape(top, rows).T
    table = table[jax.random.permutation(jax.random.fold_in(own, 1), rows)]
    offset_by = jax.random.randint(jax.random.fold_in(own, 2), (rows, 1), 0, top)
    return jnp.take_along_axis(table, (jnp.arange(top)[None, :] + offset_by) % top, axis=1)


def load_shares(number_of, total, reach, skew, full):
    weights = [(1 << 20) // math.isqrt(standing ** skew) + 1 for standing in range(1, number_of + 1)]
    largest = reach if full else min(reach, max(-(-total // number_of), total * weights[0] // sum(weights)))
    least = 1 if total - largest >= number_of - 1 else 0
    counts, spare = [largest] + [least] * (number_of - 1), total - largest - least * (number_of - 1)
    while spare > 0:
        candidates = [i for i in range(1, number_of) if counts[i] < largest] or [i for i in range(1, number_of) if counts[i] < reach]
        pool, remaining = sum([weights[i] for i in candidates]), spare
        for i in candidates:
            extra = min(reach - counts[i], max(1, remaining * weights[i] // pool), spare)
            counts[i] = counts[i] + extra
            spare = spare - extra
    return np.array(counts)


def normal_values(key, shape, deviation, limit, cuts=(), kind=jnp.bfloat16):
    level = levels(key, shape, cuts, -0.22, 0.18) if cuts else 1.0
    values = jax.random.normal(key, shape, jnp.float32) * deviation * level
    return jnp.minimum(jnp.maximum(values, -limit), limit).astype(kind)


def setup_inputs(seed: int = 0) -> dict:
    seeds = jax.random.split(jax.random.key(seed), 13)
    entry_rows = normal_values(seeds[0], (STEPS, ROWS, D), 1.0, 6.0, ((0, 2), (1, 4)))
    cache_entries = draw_cache_entries(jax.random.fold_in(seeds[12], 71), 0)
    cache_lengths = draw_cache_lengths(jax.random.fold_in(seeds[12], 71), 0)
    norm_gains = jnp.clip(1.0 + 0.18 * jax.random.normal(seeds[3], (LAYERS, 2, D), jnp.float32), 0.1, 1.9)
    expert_ids_keys = jax.random.split(jax.random.fold_in(seeds[4], 1), LAYERS * STEPS * ROWS // ROWS_DEV)
    expert_ids_turns = jax.random.permutation(jax.random.fold_in(seeds[4], 3), LAYERS * STEPS * ROWS // ROWS_DEV)
    expert_ids = jax.vmap(lambda own, number: assign_block(jax.random.fold_in(seeds[4], 2), own, number, ROWS_DEV, EXPERTS, TOP, CAP, 2))(expert_ids_keys, expert_ids_turns).reshape((LAYERS, STEPS, ROWS, TOP))
    gate_weights = jnp.clip(jnp.exp(math.log(1.0) - 2.3025851 * jax.random.uniform(seeds[5], (LAYERS, STEPS, ROWS, TOP), jnp.float32) ** levels(seeds[5], (LAYERS, STEPS, ROWS, TOP), ((0, 2), (2, 4)), -0.2, 0.2)), 0.1, 1.0)
    gate_weight = normal_values(seeds[6], (LAYERS, EXPERTS, FF, D), D ** -0.5, 0.125, ((0, 2), (1, 64)))
    up_weight = normal_values(seeds[7], (LAYERS, EXPERTS, FF, D), D ** -0.5, 0.125, ((0, 2), (1, 64)))
    down_weight = normal_values(seeds[8], (LAYERS, EXPERTS, FF, D), FF ** -0.5, 0.21875, ((0, 2), (1, 64)))
    codebook_ids = with_ends(ranked(seeds[9], (STEPS, ROWS), CODES, 2), jax.random.fold_in(seeds[9], 3), 0, CODES - 1).astype(jnp.int32)
    codec_table = normal_values(seeds[10], (CODES, D), 1.0, 6.0, ((0, 32),))
    final_gain = jnp.clip(1.0 + 0.18 * jax.random.normal(seeds[11], (D,), jnp.float32), 0.1, 1.9)
    return {"entry_rows": entry_rows, "cache_entries": cache_entries, "cache_lengths": cache_lengths, "norm_gains": norm_gains, "expert_ids": expert_ids, "gate_weights": gate_weights, "gate_weight": gate_weight, "up_weight": up_weight, "down_weight": down_weight, "codebook_ids": codebook_ids, "codec_table": codec_table, "final_gain": final_gain}


epsilon = 1e-06

def normed(values_in, gain):
    return values_in * lax.rsqrt(lax.optimization_barrier(jnp.mean(values_in * values_in, axis=-1, keepdims=True)) + epsilon) * gain

def attend_whole(hidden_in, gain, entries, lengths_now):
    head_count = D // HEAD_DIM
    groups = head_count // KV_HEADS
    rounded = lax.optimization_barrier(normed(hidden_in, gain).astype(jnp.bfloat16))
    queries = rounded.astype(jnp.float32).reshape(ROWS, KV_HEADS, groups, HEAD_DIM)
    key_rows = entries[:, 0].astype(jnp.float32).reshape(ROWS, CTX, KV_HEADS, HEAD_DIM)
    value_rows = entries[:, 1].astype(jnp.float32).reshape(ROWS, CTX, KV_HEADS, HEAD_DIM)
    scores = jnp.einsum('rkgd,rpkd->rkgp', queries, key_rows) * HEAD_DIM ** (-0.5)
    live_mask = (jnp.arange(CTX, dtype=jnp.int32)[None, :] < lengths_now[:, None])[:, None, None, :]
    scores = jnp.where(live_mask, scores, -1e+30)
    highest = lax.optimization_barrier(jnp.max(scores, axis=3, keepdims=True))
    weights = jnp.exp(scores - highest) * live_mask.astype(jnp.float32)
    weighted = jnp.einsum('rkgp,rpkd->rkgd', weights, value_rows)
    return (weighted / lax.optimization_barrier(jnp.sum(weights, axis=3))[:, :, :, None]).reshape(ROWS, D)

def expert_rows(operands):
    rows_in, gate_part, up_part, down_part = operands
    gate_out = lax.dot_general(rows_in, gate_part, (((1,), (1,)), ((), ())), preferred_element_type=jnp.float32)
    up_out = lax.dot_general(rows_in, up_part, (((1,), (1,)), ((), ())), preferred_element_type=jnp.float32)
    activ = (jax.nn.silu(gate_out) * up_out).astype(jnp.bfloat16)
    result = jnp.dot(activ, down_part, preferred_element_type=jnp.float32).astype(jnp.bfloat16)
    return result.astype(jnp.float32)

def mixture_whole(moe_in, chosen_ids, gates_now, gate_part, up_part, down_part):
    blocks = chosen_ids.reshape(N_EXPERT, ROWS_DEV * TOP)
    onehot = (blocks[:, :, None] == jnp.arange(EXPERTS, dtype=jnp.int32)[None, None, :]).astype(jnp.int32)
    before = jnp.cumsum(onehot, axis=1) - onehot
    slot_rank = lax.optimization_barrier(jnp.sum(before * onehot, axis=2)).reshape(ROWS, TOP)
    source = (jnp.arange(ROWS, dtype=jnp.int32) // ROWS_DEV)[:, None]
    slot_in = (source * CAP + slot_rank).astype(jnp.int32)
    buffer = jnp.zeros((EXPERTS, N_EXPERT * CAP, D), jnp.bfloat16)
    buffer = buffer.at[chosen_ids, slot_in].set(jnp.broadcast_to(moe_in[:, None, :], (ROWS, TOP, D)))
    results = lax.map(expert_rows, (buffer, gate_part, up_part, down_part))
    picked = results[chosen_ids, slot_in]
    gate_share = gates_now / lax.optimization_barrier(jnp.sum(gates_now, axis=1, keepdims=True))
    return lax.optimization_barrier(jnp.sum(gate_share[:, :, None] * picked, axis=1))

def reference(entry_rows, cache_entries, cache_lengths, norm_gains, expert_ids, gate_weights, gate_weight, up_weight, down_weight, codebook_ids, codec_table, final_gain):
    codec_rows = codec_table[codebook_ids].astype(jnp.float32)
    finals = []
    for step_at in range(STEPS):
        hidden_in = entry_rows[step_at].astype(jnp.float32)
        for layer_at in range(LAYERS):
            if layer_at == LAYERS // 2:
                hidden_in = hidden_in + codec_rows[step_at]
            middle = hidden_in + attend_whole(hidden_in, norm_gains[layer_at, 0], cache_entries[layer_at], cache_lengths[step_at])
            moe_in = normed(middle, norm_gains[layer_at, 1]).astype(jnp.bfloat16)
            mixed = mixture_whole(moe_in, expert_ids[layer_at, step_at], gate_weights[layer_at, step_at], gate_weight[layer_at], up_weight[layer_at], down_weight[layer_at])
            hidden_in = (middle + mixed).astype(jnp.bfloat16).astype(jnp.float32)
        finals.append(hidden_in)
    stacked = jnp.stack(finals, axis=0)
    final_rows = normed(stacked, final_gain).astype(jnp.bfloat16).reshape(STEPS * ROWS, D)
    logits = jnp.dot(final_rows, codec_table.T, preferred_element_type=jnp.float32) * D ** (-0.5)
    return logits.reshape(STEPS, ROWS, CODES)
```

```python
import functools

import jax
import jax.numpy as jnp
from jax import lax
from jax.experimental import pallas as pl
from jax.experimental.pallas import tpu as pltpu
from jax.sharding import PartitionSpec as P

F32 = jnp.float32
BF16 = jnp.bfloat16
STEPS = 4
ROWS = 8
D = 2048
HALF = D // 2
HEAD_DIM = 128
HEADS = D // HEAD_DIM
KV_HEADS = 4
GROUPS = HEADS // KV_HEADS
TOP = 8
CAP = 2
N_EXPERT = 4
N_SEQ = 16
DESTS = N_EXPERT * N_SEQ
SLOTS = STEPS * CAP
T = STEPS * ROWS
STAT = 128
PAY = HALF + STAT
PIECE = 256
EPS = 1e-6
LOWEST = -1e30


def vmem():
    return pl.BlockSpec(memory_space=pltpu.VMEM)


def smem():
    return pl.BlockSpec(memory_space=pltpu.SMEM)


def call(body, name, ins, outs, scratch=(), limit=24, flops=0, moved=0):
    return pl.pallas_call(
        body,
        name=name,
        in_specs=ins,
        out_shape=outs,
        out_specs=jax.tree.map(lambda _: vmem(), outs),
        scratch_shapes=scratch,
        compiler_params=pltpu.CompilerParams(vmem_limit_bytes=limit << 20),
        cost_estimate=pl.CostEstimate(flops=flops, bytes_accessed=moved, transcendentals=0),
    )


def shape(*dims, dtype=BF16):
    return jax.ShapeDtypeStruct(dims, dtype)


def iota(dims, axis):
    return lax.broadcasted_iota(jnp.int32, dims, axis)


def dot(a, b, dims=((1,), (0,))):
    return lax.dot_general(a, b, (dims, ((), ())), preferred_element_type=F32)


def row_order():
    to, source = iota((T, T), 0), iota((T, T), 1)
    return (source == (to % STEPS) * ROWS + to // STEPS).astype(F32).astype(BF16)


def rms(value, gain):
    return value * lax.rsqrt(jnp.mean(value * value, axis=1, keepdims=True) + EPS) * gain


def joined(section, mine, other):
    return jnp.where(
        section == 0,
        jnp.concatenate([mine, other], axis=1),
        jnp.concatenate([other, mine], axis=1),
    )


def route_body(ids_mine, ids_other, gates_mine, gates_other, books, table, hits, mixing, cod_mine, cod_other):
    section = lax.axis_index("section")
    seq = lax.axis_index("seq")
    width = DESTS * SLOTS
    column = iota((T, width), 1)
    row = iota((T, width), 0)
    same_step = (row // ROWS) == (column // CAP) % STEPS
    below, above = iota((T, T), 0), iota((T, T), 1)
    earlier = ((below // ROWS == above // ROWS) & (above < below)).astype(F32).astype(BF16)
    order = row_order()
    for layer in range(2):
        ids = jnp.where(section == layer, ids_mine[0], ids_other[0]).reshape(T, TOP)
        gates = jnp.where(section == layer, gates_mine[0], gates_other[0]).reshape(T, TOP)
        shares = gates / jnp.sum(gates, axis=1, keepdims=True)
        named = jnp.zeros((T, width), F32)
        weight = jnp.zeros((T, width), F32)
        for k in range(TOP):
            match = (ids[:, k : k + 1] == column // SLOTS) & same_step
            named = jnp.where(match, 1.0, named)
            weight = jnp.where(match, shares[:, k : k + 1], weight)
        rank = dot(earlier, named.astype(BF16))
        keep = rank == (column % CAP).astype(F32)
        hit = jnp.where(keep, named, 0.0)
        share = jnp.where(keep, weight, 0.0)
        high = share.astype(BF16)
        low = (share - high.astype(F32)).astype(BF16)
        hits[layer] = dot(order, hit.astype(BF16)).astype(BF16)
        mixing[layer, :T] = dot(order, high).astype(BF16)
        mixing[layer, T:] = dot(order, low).astype(BF16)
    codes = table.shape[0]
    line = iota((T, codes), 0)
    wanted = jnp.zeros((T, codes), jnp.int32)
    for row_at in range(ROWS):
        for step in range(STEPS):
            wanted = jnp.where(line == row_at * STEPS + step, books[step, row_at], wanted)
    start = (section * N_SEQ + seq) * codes
    picked = (wanted - start == iota((T, codes), 1)).astype(F32).astype(BF16)
    part = dot(picked, table[...])
    first, second = part[:, :HALF], part[:, HALF:]
    cod_mine[...] = jnp.where(section == 0, first, second).astype(BF16)
    cod_other[...] = jnp.where(section == 0, second, first).astype(BF16)


def attend_body(entering, lengths, part_a, part_b, gains, cache, mine, other, kv, queries, values, stats, sems):
    section = lax.axis_index("section")
    seq = lax.axis_index("seq")
    ctx = kv.shape[2]
    copies = [pltpu.make_async_copy(cache.at[0, r], kv.at[r], sems.at[r]) for r in range(ROWS)]
    for copy in copies:
        copy.start()
    if entering:
        a = part_a[...].astype(F32).reshape(T // 2, D)
        b = part_b[...].astype(F32).reshape(T // 2, D)
        rows = jnp.where(section == 0, jnp.concatenate([a, b], axis=0), jnp.concatenate([b, a], axis=0))
        hidden = dot(row_order(), rows.astype(BF16))
    else:
        hidden = joined(section, part_a[...], part_b[...])
    normed = rms(hidden, gains[0, 0:1, :])
    values[...] = hidden
    for r in range(ROWS):
        for h in range(HEADS):
            at = (h % GROUPS) * STEPS
            queries[r, h // GROUPS, at : at + STEPS, :] = normed[
                r * STEPS : (r + 1) * STEPS, h * HEAD_DIM : (h + 1) * HEAD_DIM
            ]
    lines = GROUPS * STEPS
    step_of = iota((KV_HEADS * lines, ctx), 0) % STEPS
    position = seq * ctx + iota((KV_HEADS * lines, ctx), 1)
    lane = iota((STEPS, STAT), 1)
    for r in range(ROWS):
        copies[r].wait()
        scores = jnp.concatenate(
            [
                dot(
                    queries[r, k].astype(BF16),
                    kv[r, 0, :, k * HEAD_DIM : (k + 1) * HEAD_DIM],
                    ((1,), (1,)),
                )
                for k in range(KV_HEADS)
            ],
            axis=0,
        ) * HEAD_DIM ** (-0.5)
        limit = jnp.zeros_like(step_of)
        for step in range(STEPS):
            limit = jnp.where(step_of == step, lengths[step, r], limit)
        live = position < limit
        scores = jnp.where(live, scores, LOWEST)
        highest = jnp.max(scores, axis=1, keepdims=True)
        weights = jnp.where(live, jnp.exp(scores - highest), 0.0)
        total = jnp.sum(weights, axis=1, keepdims=True)
        some = total > 0.0
        safe = jnp.where(some, total, 1.0)
        log_sum = jnp.where(some, highest + jnp.log(safe), LOWEST)
        scaled = 1.0 / safe
        weights = weights.astype(BF16)
        line_stats = jnp.zeros((STEPS, STAT), F32)
        for k in range(KV_HEADS):
            span = slice(k * lines, (k + 1) * lines)
            out = dot(weights[span], kv[r, 1, :, k * HEAD_DIM : (k + 1) * HEAD_DIM]) * scaled[span]
            logs = jnp.broadcast_to(log_sum[span], (lines, STAT))
            for g in range(GROUPS):
                h = k * GROUPS + g
                at = slice(g * STEPS, (g + 1) * STEPS)
                rows_at = slice(r * STEPS, (r + 1) * STEPS)
                lanes_at = slice(h * HEAD_DIM, (h + 1) * HEAD_DIM)
                values[rows_at, lanes_at] = values[rows_at, lanes_at] + out[at]
                line_stats = jnp.where(lane == h, logs[at], line_stats)
        stats[r * STEPS : (r + 1) * STEPS, :] = line_stats
    logs = stats[...]
    high = logs.astype(BF16).astype(F32)
    mid = (logs - high).astype(BF16).astype(F32)
    low = (logs - high - mid).astype(BF16).astype(F32)
    lane = iota((T, STAT), 1)
    half = HEADS // 2

    def block(second):
        def moved(value, by):
            by = (by - (half if second else 0)) % STAT
            return pltpu.roll(value, by, 1) if by else value

        packed = jnp.where(lane < 2 * half, moved(mid, half), moved(low, 2 * half))
        return jnp.where(lane < half, moved(high, 0), packed)

    is_first = section == 0
    mine[:, :HALF] = jnp.where(is_first, values[:, :HALF], values[:, HALF:]).astype(BF16)
    other[:, :HALF] = jnp.where(is_first, values[:, HALF:], values[:, :HALF]).astype(BF16)
    first, second = block(False), block(True)
    mine[:, HALF:] = jnp.where(is_first, first, second).astype(BF16)
    other[:, HALF:] = jnp.where(is_first, second, first).astype(BF16)


def spread_body(layer, mine, got, hits, *rest):
    out = rest[-1]
    section = lax.axis_index("section")
    expert = lax.axis_index("expert")
    active = section == layer
    use = jnp.where(active, mine[...].astype(F32), got[...].astype(F32)).astype(BF16)
    pick = hits[layer]
    for at in range(0, PAY, 384):
        out[:, at : at + 384] = dot(pick, use[:, at : at + 384], ((0,), (0,))).astype(BF16)
    if layer == 0:
        codes = rest[0][...].astype(F32) + rest[1][...].astype(F32)
        for s in range(0, N_SEQ, 2):
            rows_at = slice((s // 4) * ROWS, (s // 4 + 1) * ROWS)
            pair = jnp.concatenate(
                [codes[rows_at, (q % 4) * PIECE : (q % 4 + 1) * PIECE] for q in (s, s + 1)], axis=0
            )
            for x in range(N_EXPERT):
                at = (x * N_SEQ + s) * SLOTS
                out[at : at + 2 * SLOTS, PAY:] = jnp.where(expert == x, pair, 0.0).astype(BF16)


def combine_body(layer, got, *outs):
    middle = outs[0]
    half = HEADS // 2
    block = N_SEQ * SLOTS
    for x in range(N_EXPERT):
        rows_at = slice(x * block, (x + 1) * block)
        packed = got[rows_at, HALF:PAY].astype(F32)
        logs = packed[:, :half] + packed[:, half : 2 * half] + packed[:, 2 * half : 3 * half]
        logs = logs.reshape(N_SEQ, SLOTS, half)
        weights = jnp.exp(logs - jnp.max(logs, axis=0, keepdims=True))
        weights = weights / jnp.sum(weights, axis=0, keepdims=True)
        for h in range(half):
            lanes_at = slice(h * HEAD_DIM, (h + 1) * HEAD_DIM)
            part = got[rows_at, lanes_at].astype(F32).reshape(N_SEQ, SLOTS, HEAD_DIM)
            middle[x * SLOTS : (x + 1) * SLOTS, lanes_at] = jnp.sum(part * weights[:, :, h : h + 1], axis=0)
    if layer == 0:
        codes = got[:, PAY:].astype(F32).reshape(DESTS, SLOTS, PIECE)
        outs[1][...] = jnp.sum(codes, axis=0)


def expert_body(mid_mine, mid_got, gains, gate, up, down, mine, other, gate_v, up_v, down_v, sems):
    section = lax.axis_index("section")
    ff = gate_v.shape[0]
    chunks = sems.shape[1]
    size = ff // chunks
    copies = {}
    for j in range(chunks):
        at = pl.ds(j * size, size)
        for i, (source, target) in enumerate(((gate, gate_v), (up, up_v))):
            copies[i, j] = pltpu.make_async_copy(source.at[0, 0, at], target.at[at], sems.at[i, j])
    for j in range(chunks):
        at = pl.ds(j * size, size)
        copies[2, j] = pltpu.make_async_copy(down.at[0, 0, at], down_v.at[at], sems.at[2, j])
    for copy in copies.values():
        copy.start()
    middle = joined(section, mid_mine[...], mid_got[...])
    moe_in = rms(middle, gains[0, 1:2, :]).astype(BF16)
    activ = []
    for j in range(chunks):
        at = slice(j * size, (j + 1) * size)
        copies[0, j].wait()
        gate_out = dot(moe_in, gate_v[at], ((1,), (1,)))
        copies[1, j].wait()
        up_out = dot(moe_in, up_v[at], ((1,), (1,)))
        activ.append((gate_out / (1.0 + jnp.exp(-gate_out)) * up_out).astype(BF16))
    total = jnp.zeros((T, D), F32)
    for j in range(chunks):
        at = slice(j * size, (j + 1) * size)
        copies[2, j].wait()
        total = total + dot(activ[j], down_v[at])
    result = total.astype(BF16).astype(F32) + middle
    first, second = result[:, :HALF], result[:, HALF:]
    mine[...] = jnp.where(section == 0, first, second).astype(BF16)
    other[...] = jnp.where(section == 0, second, first).astype(BF16)


def share_body(layer, mine, got, *rest):
    out = rest[-1]
    section = lax.axis_index("section")
    expert = lax.axis_index("expert")
    use = jnp.where(section == layer, mine[...].astype(F32), got[...].astype(F32))
    for x in range(N_EXPERT):
        rows = use[x * SLOTS : (x + 1) * SLOTS]
        pair = jnp.concatenate([rows, rows], axis=0).astype(BF16)
        if layer == 0:
            piece = jnp.where(expert == x, rest[0][...], 0.0)
            codes = jnp.concatenate([piece, piece], axis=0).astype(BF16)
        for s in range(0, N_SEQ, 2):
            at = (x * N_SEQ + s) * SLOTS
            out[at : at + 2 * SLOTS, :HALF] = pair
            if layer == 0:
                out[at : at + 2 * SLOTS, HALF:] = codes


def mix_body(layer, got, mixing, out):
    both = dot(mixing[layer], got[:, :HALF])
    hidden = (both[:T] + both[T:]).astype(BF16).astype(F32)
    if layer == 0:
        codes = got[:, HALF:].astype(F32).reshape(N_EXPERT, N_SEQ, SLOTS, PIECE)
        codes = jnp.sum(codes, axis=0)
        for s in range(N_SEQ):
            rows_at = slice((s // 4) * ROWS, (s // 4 + 1) * ROWS)
            lanes_at = slice((s % 4) * PIECE, (s % 4 + 1) * PIECE)
            out[rows_at, lanes_at] = hidden[rows_at, lanes_at] + codes[s]
    else:
        out[...] = hidden


def head_body(mine, got, gain, table, out):
    hidden = joined(lax.axis_index("section"), mine[...], got[...])
    final = rms(hidden, gain[...]).astype(BF16)
    final = dot(row_order(), final, ((0,), (0,))).astype(BF16)
    logits = dot(final, table[...], ((1,), (1,))) * D ** (-0.5)
    out[...] = logits.reshape(out.shape)


def swapped(value):
    return lax.ppermute(value, "section", [(0, 1), (1, 0)])


def exchanged(value):
    return lax.all_to_all(value, ("expert", "seq"), 0, 0, tiled=True)


def per_device(
    entry_rows,
    cache_entries,
    cache_lengths,
    norm_gains,
    expert_ids,
    gate_weights,
    gate_weight,
    up_weight,
    down_weight,
    codebook_ids,
    codec_table,
    final_gain,
):
    ctx = cache_entries.shape[3]
    kv_width = cache_entries.shape[4]
    ff = gate_weight.shape[2]
    codes = codec_table.shape[0]
    anywhere = pl.BlockSpec(memory_space=pl.ANY)
    entry_got = swapped(entry_rows)
    ids_got = swapped(expert_ids)
    gates_got = swapped(gate_weights)
    hits, mixing, cod_mine, cod_other = call(
        route_body,
        "route",
        [vmem()] * 4 + [smem(), vmem()],
        (
            shape(2, T, DESTS * SLOTS),
            shape(2, 2 * T, DESTS * SLOTS),
            shape(T, HALF),
            shape(T, HALF),
        ),
    )(expert_ids, ids_got, gate_weights, gates_got, codebook_ids, codec_table)
    cod_got = swapped(cod_other)
    part_a, part_b = entry_rows, entry_got
    for layer in range(2):
        first = layer == 0
        mine, other = call(
            functools.partial(attend_body, first),
            "attend",
            [smem(), vmem(), vmem(), vmem(), anywhere],
            (shape(T, PAY), shape(T, PAY)),
            [
                pltpu.VMEM((ROWS, 2, ctx, kv_width), BF16),
                pltpu.VMEM((ROWS, KV_HEADS, GROUPS * STEPS, HEAD_DIM), F32),
                pltpu.VMEM((T, D), F32),
                pltpu.VMEM((T, STAT), F32),
                pltpu.SemaphoreType.DMA((ROWS,)),
            ],
        )(cache_lengths, part_a, part_b, norm_gains, cache_entries)
        codec_in = (cod_mine, cod_got) if first else ()
        width = PAY + PIECE if first else PAY
        sent = call(
            functools.partial(spread_body, layer),
            "spread",
            [vmem()] * (3 + len(codec_in)),
            shape(DESTS * SLOTS, width),
        )(mine, swapped(other), hits, *codec_in)
        outs = (shape(T, HALF, dtype=F32), shape(SLOTS, PIECE, dtype=F32))
        combined = call(
            functools.partial(combine_body, layer),
            "combine",
            [vmem()],
            outs if first else outs[:1],
        )(exchanged(sent))
        middle = combined[0]
        mine, other = call(
            expert_body,
            "experts",
            [vmem()] * 3 + [anywhere] * 3,
            (shape(T, HALF), shape(T, HALF)),
            [pltpu.VMEM((ff, D), BF16)] * 3 + [pltpu.SemaphoreType.DMA((3, 3))],
            limit=32,
        )(middle, swapped(middle), norm_gains, gate_weight, up_weight, down_weight)
        pieces = combined[1:]
        sent = call(
            functools.partial(share_body, layer),
            "share",
            [vmem()] * (2 + len(pieces)),
            shape(DESTS * SLOTS, HALF + PIECE if first else HALF),
        )(mine, swapped(other), *pieces)
        part_a = call(
            functools.partial(mix_body, layer),
            "mix",
            [vmem()] * 2,
            shape(T, HALF, dtype=F32),
        )(exchanged(sent), mixing)
        part_b = swapped(part_a)
    return call(
        head_body,
        "head",
        [vmem()] * 4,
        shape(STEPS, ROWS, codes, dtype=F32),
    )(part_a, part_b, final_gain.reshape(1, D), codec_table)


def solution(mesh):
    placed = (
        P("section", "expert", None),
        P("section", "expert", None, "seq", None),
        P(None, "expert"),
        P("section", None, None),
        P("section", None, "expert", None),
        P("section", None, "expert", None),
        P("section", ("expert", "seq"), None, None),
        P("section", ("expert", "seq"), None, None),
        P("section", ("expert", "seq"), None, None),
        P(None, "expert"),
        P(("section", "seq"), None),
        P(),
    )
    return jax.shard_map(
        per_device,
        mesh=mesh,
        in_specs=placed,
        out_specs=P(None, "expert", ("section", "seq")),
        check_vma=False,
    )
```

```python
import functools

import jax
import jax.numpy as jnp
from jax import lax
from jax.experimental import pallas as pl
from jax.experimental.pallas import tpu as pltpu
from jax.sharding import PartitionSpec as P

F32 = jnp.float32
BF16 = jnp.bfloat16
STEPS = 4
ROWS = 8
D = 2048
HALF = D // 2
HEAD_DIM = 128
HEADS = D // HEAD_DIM
KV_HEADS = 4
GROUPS = HEADS // KV_HEADS
TOP = 8
CAP = 2
N_EXPERT = 4
N_SEQ = 16
DESTS = N_EXPERT * N_SEQ
SLOTS = STEPS * CAP
T = STEPS * ROWS
STAT = 128
PAY = HALF + STAT
PIECE = HALF // N_SEQ
EPS = 1e-6
LOWEST = -1e30


def vmem():
    return pl.BlockSpec(memory_space=pltpu.VMEM)


def hbm():
    return pl.BlockSpec(memory_space=pltpu.HBM)


def smem():
    return pl.BlockSpec(memory_space=pltpu.SMEM)


def call(body, name, ins, outs, scratch=(), limit=24):
    return pl.pallas_call(
        body,
        name=name,
        in_specs=ins,
        out_shape=outs,
        out_specs=jax.tree.map(lambda _: vmem(), outs),
        scratch_shapes=scratch,
        compiler_params=pltpu.CompilerParams(vmem_limit_bytes=limit << 20),
    )


def shape(*dims, dtype=BF16):
    return jax.ShapeDtypeStruct(dims, dtype)


def iota(dims, axis):
    return lax.broadcasted_iota(jnp.int32, dims, axis)


def dot(a, b, dims=((1,), (0,))):
    return lax.dot_general(a, b, (dims, ((), ())), preferred_element_type=F32)


def row_order():
    to, source = iota((T, T), 0), iota((T, T), 1)
    return (source == (to % STEPS) * ROWS + to // STEPS).astype(F32).astype(BF16)


def rms(value, gain):
    return value * lax.rsqrt(jnp.mean(value * value, axis=1, keepdims=True) + EPS) * gain


def joined(section, mine, other):
    return jnp.where(
        section == 0,
        jnp.concatenate([mine, other], axis=1),
        jnp.concatenate([other, mine], axis=1),
    )


def placed_rows(section, layer, ids_mine, ids_other, gates_mine, gates_other, hits, mixing):
    width = DESTS * SLOTS
    column = iota((T, width), 1)
    row = iota((T, width), 0)
    same_step = (row // ROWS) == (column // CAP) % STEPS
    below, above = iota((T, T), 0), iota((T, T), 1)
    earlier = ((below // ROWS == above // ROWS) & (above < below)).astype(F32).astype(BF16)
    order = row_order()
    ids = jnp.where(section == layer, ids_mine[0], ids_other[0]).reshape(T, TOP)
    gates = jnp.where(section == layer, gates_mine[0], gates_other[0]).reshape(T, TOP)
    shares = gates / jnp.sum(gates, axis=1, keepdims=True)
    named = jnp.zeros((T, width), F32)
    weight = jnp.zeros((T, width), F32)
    for k in range(TOP):
        match = (ids[:, k : k + 1] == column // SLOTS) & same_step
        named = jnp.where(match, 1.0, named)
        weight = jnp.where(match, shares[:, k : k + 1], weight)
    rank = dot(earlier, named.astype(BF16))
    keep = rank == (column % CAP).astype(F32)
    hit = jnp.where(keep, named, 0.0)
    share = jnp.where(keep, weight, 0.0)
    high = share.astype(BF16)
    low = (share - high.astype(F32)).astype(BF16)
    hits[layer] = dot(order, hit.astype(BF16)).astype(BF16)
    mixing[layer, :T] = dot(order, high).astype(BF16)
    mixing[layer, T:] = dot(order, low).astype(BF16)


def codec_part(section, seq, books, table):
    codes = table.shape[0]
    line = iota((T, codes), 0)
    wanted = jnp.zeros((T, codes), jnp.int32)
    for row_at in range(ROWS):
        for step in range(STEPS):
            wanted = jnp.where(line == row_at * STEPS + step, books[step, row_at], wanted)
    start = (section * N_SEQ + seq) * codes
    picked = (wanted - start == iota((T, codes), 1)).astype(F32).astype(BF16)
    return dot(picked, table[...])


def lay_queries(hidden, gain, queries, values):
    normed = rms(hidden, gain)
    values[...] = hidden
    queries[...] = jnp.zeros_like(queries)
    for r in range(ROWS):
        for h in range(HEADS):
            k = h // GROUPS
            at = h * STEPS
            queries[r, at : at + STEPS, k * HEAD_DIM : (k + 1) * HEAD_DIM] = normed[
                r * STEPS : (r + 1) * STEPS, h * HEAD_DIM : (h + 1) * HEAD_DIM
            ]


def attend_rows(seq, lengths, cache_row, queries, values, stats, scores, weights):
    lines = GROUPS * STEPS
    size = HEADS * STEPS
    ctx = scores.shape[1]
    lane = iota((STEPS, STAT), 1)
    step_of = iota((size, ctx), 0) % STEPS
    position = seq * ctx + iota((size, ctx), 1)
    for r in range(ROWS):
        keys, _ = cache_row(r)
        scores[r * size : (r + 1) * size] = dot(queries[r].astype(BF16), keys, ((1,), (1,)))
    scales = []
    for r in range(ROWS):
        limit = jnp.where(step_of == 0, lengths[0, r], 0)
        for step in range(1, STEPS):
            limit = jnp.where(step_of == step, lengths[step, r], limit)
        live = position < limit
        score = jnp.where(live, scores[r * size : (r + 1) * size] * HEAD_DIM ** (-0.5), LOWEST)
        highest = jnp.max(score, axis=1, keepdims=True)
        weight = jnp.where(live, jnp.exp(score - highest), 0.0)
        total = jnp.sum(weight, axis=1, keepdims=True)
        some = total > 0.0
        safe = jnp.where(some, total, 1.0)
        log_sum = jnp.where(some, highest + jnp.log(safe), LOWEST)
        scales.append(1.0 / safe)
        weights[r * size : (r + 1) * size] = weight.astype(BF16)
        logs = jnp.broadcast_to(log_sum, (size, STAT))
        line_stats = jnp.zeros((STEPS, STAT), F32)
        for h in range(HEADS):
            line_stats = jnp.where(lane == h, logs[h * STEPS : (h + 1) * STEPS], line_stats)
        stats[r * STEPS : (r + 1) * STEPS, :] = line_stats
    for r in range(ROWS):
        _, held = cache_row(r)
        outs = dot(weights[r * size : (r + 1) * size], held)
        rows_at = slice(r * STEPS, (r + 1) * STEPS)
        for k in range(KV_HEADS):
            span = slice(k * lines, (k + 1) * lines)
            out = outs[span, k * HEAD_DIM : (k + 1) * HEAD_DIM] * scales[r][span]
            for g in range(GROUPS):
                h = k * GROUPS + g
                lanes_at = slice(h * HEAD_DIM, (h + 1) * HEAD_DIM)
                values[rows_at, lanes_at] = values[rows_at, lanes_at] + out[g * STEPS : (g + 1) * STEPS]


def pack_halves(section, values, stats, mine, other):
    logs = stats[...]
    high = logs.astype(BF16).astype(F32)
    mid = (logs - high).astype(BF16).astype(F32)
    low = (logs - high - mid).astype(BF16).astype(F32)
    lane = iota((T, STAT), 1)
    half = HEADS // 2

    def block(second):
        def moved(value, by):
            by = (by - (half if second else 0)) % STAT
            return pltpu.roll(value, by, 1) if by else value

        packed = jnp.where(lane < 2 * half, moved(mid, half), moved(low, 2 * half))
        return jnp.where(lane < half, moved(high, 0), jnp.where(lane < 3 * half, packed, 0.0))

    is_first = section == 0
    mine[:, :HALF] = jnp.where(is_first, values[:, :HALF], values[:, HALF:]).astype(BF16)
    other[:, :HALF] = jnp.where(is_first, values[:, HALF:], values[:, :HALF]).astype(BF16)
    first, second = block(False), block(True)
    mine[:, HALF:PAY] = jnp.where(is_first, first, second).astype(BF16)
    other[:, HALF:PAY] = jnp.where(is_first, second, first).astype(BF16)


def enter_body(
    ids_in, ids_got, gates_in, gates_got, books_in, lengths_in, table_in, entry_in, entry_got, gains_in, cache,
    mine, other, hits, mixing,
    ids, gates, books, lengths, table, entry, gains, kv, queries, values, stats, scores, weights, small_sems, sems,
):
    section = lax.axis_index("section")
    seq = lax.axis_index("seq")
    small = [
        pltpu.make_async_copy(source, target, small_sems.at[i])
        for i, (source, target) in enumerate(
            (
                (entry_in, entry),
                (gains_in, gains),
                (ids_in, ids),
                (gates_in, gates),
                (books_in, books),
                (lengths_in, lengths),
                (table_in, table),
            )
        )
    ]
    copies = [pltpu.make_async_copy(cache.at[0, r], kv.at[r], sems.at[r]) for r in range(ROWS)]
    for copy in small + copies:
        copy.start()
    for copy in small:
        copy.wait()
    for layer in range(2):
        placed_rows(section, layer, ids, ids_got, gates, gates_got, hits, mixing)
    codes = codec_part(section, seq, books, table)
    first, second = codes[:, :HALF], codes[:, HALF:]
    mine[:, PAY:] = jnp.where(section == 0, first, second).astype(BF16)
    other[:, PAY:] = jnp.where(section == 0, second, first).astype(BF16)
    a = entry[...].astype(F32).reshape(T // 2, D)
    b = entry_got[...].astype(F32).reshape(T // 2, D)
    rows = jnp.where(section == 0, jnp.concatenate([a, b], axis=0), jnp.concatenate([b, a], axis=0))
    lay_queries(dot(row_order(), rows.astype(BF16)), gains[0, 0:1, :], queries, values)

    for copy in copies:
        copy.wait()
    attend_rows(seq, lengths, lambda r: (kv[r, 0], kv[r, 1]), queries, values, stats, scores, weights)
    pack_halves(section, values, stats, mine, other)


def attend_body(lengths, part_a, part_b, gains, cache, mine, other, queries, values, stats, scores, weights):
    section = lax.axis_index("section")
    lay_queries(joined(section, part_a[...], part_b[...]), gains[0, 0:1, :], queries, values)
    seq = lax.axis_index("seq")
    attend_rows(
        seq, lengths, lambda r: (cache[0, r, 0], cache[0, r, 1]), queries, values, stats, scores, weights
    )
    pack_halves(section, values, stats, mine, other)


def spread_body(layer, mine, got, hits, held):
    section = lax.axis_index("section")
    pick = hits[layer]
    use = jnp.where(section == layer, mine[...].astype(F32), got[...].astype(F32)).astype(BF16)
    for at in range(0, HALF, 512):
        held[:, at : at + 512] = dot(pick, use[:, at : at + 512], ((0,), (0,))).astype(BF16)
    last = dot(pick, use[:, HALF:PAY], ((0,), (0,)))
    if layer == 0:
        codes = mine[:, PAY:].astype(F32) + got[:, PAY:].astype(F32)
        tiles = []
        for x in range(N_EXPERT):
            for s in range(0, HALF, STAT):
                tile = codes[x * SLOTS : (x + 1) * SLOTS, s : s + STAT]
                tiles += [pltpu.roll(tile, PIECE, 1), tile]
        last = jnp.where(iota(last.shape, 1) < STAT - PIECE, last, jnp.concatenate(tiles, axis=0))
    held[:, HALF:PAY] = last.astype(BF16)


def combine_body(layer, got, *outs):
    middle = outs[0]
    half = HEADS // 2
    block = N_SEQ * SLOTS
    widen = (iota((STAT, HALF), 0) == iota((STAT, HALF), 1) // HEAD_DIM).astype(F32).astype(BF16)
    for x in range(N_EXPERT):
        rows_at = slice(x * block, (x + 1) * block)
        packed = got[rows_at, HALF:PAY].astype(F32)
        logs = packed + pltpu.roll(packed, STAT - half, 1) + pltpu.roll(packed, STAT - 2 * half, 1)
        logs = logs.reshape(N_SEQ, SLOTS, STAT)
        weights = jnp.exp(logs - jnp.max(logs, axis=0, keepdims=True))
        weights = weights / jnp.sum(weights, axis=0, keepdims=True)
        weights = weights.reshape(block, STAT)
        high = weights.astype(BF16)
        low = (weights - high.astype(F32)).astype(BF16)
        wide = dot(high, widen) + dot(low, widen)
        for at in range(0, HALF, 256):
            lanes_at = slice(at, at + 256)
            part = (got[rows_at, lanes_at].astype(F32) * wide[:, lanes_at]).reshape(N_SEQ, SLOTS, 256)
            middle[x * SLOTS : (x + 1) * SLOTS, lanes_at] = jnp.sum(part, axis=0)
        if layer == 0:
            outs[1][x * SLOTS : (x + 1) * SLOTS, :] = jnp.sum(packed.reshape(N_SEQ, SLOTS, STAT), axis=0)


def expert_body(mid_mine, mid_got, gains, gate, up, down, mine, other):
    section = lax.axis_index("section")
    ff = gate.shape[2]
    size = 256
    middle = joined(section, mid_mine[...], mid_got[...])
    moe_in = rms(middle, gains[0, 1:2, :]).astype(BF16)
    total = jnp.zeros((T, D), F32)
    for j in range(0, ff, size):
        at = slice(j, j + size)
        gate_out = dot(moe_in, gate[0, 0, at, :], ((1,), (1,)))
        up_out = dot(moe_in, up[0, 0, at, :], ((1,), (1,)))
        activ = (gate_out / (1.0 + jnp.exp(-gate_out)) * up_out).astype(BF16)
        total = total + dot(activ, down[0, 0, at, :])
    result = total.astype(BF16).astype(F32) + middle
    first, second = result[:, :HALF], result[:, HALF:]
    mine[...] = jnp.where(section == 0, first, second).astype(BF16)
    other[...] = jnp.where(section == 0, second, first).astype(BF16)


def share_body(layer, mine, got, *rest):
    held = rest[-1]
    section = lax.axis_index("section")
    use = jnp.where(section == layer, mine[...].astype(F32), got[...].astype(F32))
    if layer == 0:
        use = jnp.concatenate([use, rest[0][...]], axis=1)
    for x in range(N_EXPERT):
        rows = use[x * SLOTS : (x + 1) * SLOTS]
        pair = jnp.concatenate([rows, rows], axis=0).astype(BF16)
        for s in range(0, N_SEQ, 2):
            at = (x * N_SEQ + s) * SLOTS
            held[at : at + 2 * SLOTS, :] = pair


def mix_body(layer, got, mixing, out):
    both = dot(mixing[layer], got[:, :HALF])
    hidden = (both[:T] + both[T:]).astype(BF16).astype(F32)
    if layer == 0:
        codes = got[:, HALF:].astype(F32)
        lower = iota((SLOTS, STAT), 1) < PIECE
        for x in range(N_EXPERT):
            rows_at = slice(x * SLOTS, (x + 1) * SLOTS)
            for s in range(0, N_SEQ, 2):
                at = (x * N_SEQ + s) * SLOTS
                even, odd = codes[at : at + SLOTS], codes[at + SLOTS : at + 2 * SLOTS]
                lanes_at = slice(s * PIECE, (s + 2) * PIECE)
                tile = jnp.where(lower, pltpu.roll(even, PIECE, 1), odd)
                out[rows_at, lanes_at] = hidden[rows_at, lanes_at] + tile
    else:
        out[...] = hidden


def head_body(mine, got, gain, table, out):
    hidden = joined(lax.axis_index("section"), mine[...], got[...])
    final = rms(hidden, gain[...]).astype(BF16)
    final = dot(row_order(), final, ((0,), (0,))).astype(BF16)
    logits = dot(final, table[...], ((1,), (1,))) * D ** (-0.5)
    out[...] = logits.reshape(out.shape)


def swapped(value):
    return lax.ppermute(value, "section", [(0, 1), (1, 0)])


def in_hbm(value):
    return pltpu.with_memory_space_constraint(value, pltpu.HBM)


def exchanged(value):
    return lax.all_to_all(value, ("expert", "seq"), 0, 0, tiled=True)


def per_device(
    entry_rows,
    cache_entries,
    cache_lengths,
    norm_gains,
    expert_ids,
    gate_weights,
    gate_weight,
    up_weight,
    down_weight,
    codebook_ids,
    codec_table,
    final_gain,
):
    ctx = cache_entries.shape[3]
    kv_width = cache_entries.shape[4]
    codes = codec_table.shape[0]
    attention_scratch = [
        pltpu.VMEM((ROWS, HEADS * STEPS, kv_width), F32),
        pltpu.VMEM((T, D), F32),
        pltpu.VMEM((T, STAT), F32),
        pltpu.VMEM((ROWS * HEADS * STEPS, ctx), F32),
        pltpu.VMEM((ROWS * HEADS * STEPS, ctx), BF16),
    ]
    entry_got, ids_got, gates_got = swapped(entry_rows), swapped(expert_ids), swapped(gate_weights)
    mine, other, hits, mixing = call(
        enter_body,
        "enter",
        [hbm(), vmem()] * 2 + [hbm()] * 4 + [vmem()] + [hbm()] * 2,
        (
            shape(T, PAY + HALF),
            shape(T, PAY + HALF),
            shape(2, T, DESTS * SLOTS),
            shape(2, 2 * T, DESTS * SLOTS),
        ),
        [
            pltpu.VMEM(expert_ids.shape, jnp.int32),
            pltpu.VMEM(gate_weights.shape, F32),
            pltpu.SMEM(codebook_ids.shape, jnp.int32),
            pltpu.SMEM(cache_lengths.shape, jnp.int32),
            pltpu.VMEM(codec_table.shape, BF16),
            pltpu.VMEM(entry_rows.shape, BF16),
            pltpu.VMEM(norm_gains.shape, F32),
            pltpu.VMEM((ROWS, 2, ctx, kv_width), BF16),
            *attention_scratch,
            pltpu.SemaphoreType.DMA((7,)),
            pltpu.SemaphoreType.DMA((ROWS,)),
        ],
    )(
        in_hbm(expert_ids),
        ids_got,
        in_hbm(gate_weights),
        gates_got,
        in_hbm(codebook_ids),
        in_hbm(cache_lengths),
        in_hbm(codec_table),
        in_hbm(entry_rows),
        entry_got,
        in_hbm(norm_gains),
        in_hbm(cache_entries),
    )
    for layer in range(2):
        first = layer == 0
        if not first:
            mine, other = call(
                attend_body,
                "attend",
                [smem()] + [vmem()] * 4,
                (shape(T, PAY), shape(T, PAY)),
                attention_scratch,
            )(cache_lengths, part_a, part_b, norm_gains, cache_entries)
        sent = call(
            functools.partial(spread_body, layer),
            "spread",
            [vmem()] * 3,
            shape(DESTS * SLOTS, PAY),
        )(mine, swapped(other), hits)
        outs = (shape(T, HALF, dtype=F32), shape(T, STAT, dtype=F32))
        combined = call(
            functools.partial(combine_body, layer),
            "combine",
            [vmem()],
            outs if first else outs[:1],
        )(exchanged(sent))
        middle = combined[0]
        mine, other = call(
            expert_body,
            "experts",
            [vmem()] * 6,
            (shape(T, HALF), shape(T, HALF)),
        )(middle, swapped(middle), norm_gains, gate_weight, up_weight, down_weight)
        pieces = combined[1:]
        width = PAY if first else HALF
        sent = call(
            functools.partial(share_body, layer),
            "share",
            [vmem()] * (2 + len(pieces)),
            shape(DESTS * SLOTS, width),
        )(mine, swapped(other), *pieces)
        part_a = call(
            functools.partial(mix_body, layer),
            "mix",
            [vmem()] * 2,
            shape(T, HALF, dtype=F32),
        )(exchanged(sent), mixing)
        part_b = swapped(part_a)
    return call(
        head_body,
        "head",
        [vmem()] * 4,
        shape(STEPS, ROWS, codes, dtype=F32),
    )(part_a, part_b, final_gain.reshape(1, D), codec_table)


def solution(mesh):
    placed = (
        P("section", "expert", None),
        P("section", "expert", None, "seq", None),
        P(None, "expert"),
        P("section", None, None),
        P("section", None, "expert", None),
        P("section", None, "expert", None),
        P("section", ("expert", "seq"), None, None),
        P("section", ("expert", "seq"), None, None),
        P("section", ("expert", "seq"), None, None),
        P(None, "expert"),
        P(("section", "seq"), None),
        P(),
    )
    return jax.shard_map(
        per_device,
        mesh=mesh,
        in_specs=placed,
        out_specs=P(None, "expert", ("section", "seq")),
        check_vma=False,
    )
```

```python
import functools

import jax
import jax.numpy as jnp
from jax import lax
from jax.experimental import pallas as pl
from jax.experimental.pallas import tpu as pltpu
from jax.sharding import PartitionSpec as P

F32 = jnp.float32
BF16 = jnp.bfloat16
STEPS = 4
ROWS = 8
D = 2048
HEAD_DIM = 128
HEADS = D // HEAD_DIM
KV_HEADS = 4
GROUPS = HEADS // KV_HEADS
TOP = 8
CAP = 2
N_EXPERT = 4
N_SEQ = 16
DESTS = N_EXPERT * N_SEQ
SLOTS = STEPS * CAP
T = STEPS * ROWS
STAT = 128
PAY = D + STAT
PIECE = D // 4
CHUNKS = 3
EPS = 1e-6
LOWEST = -1e30


def vmem():
    return pl.BlockSpec(memory_space=pltpu.VMEM)


def hbm():
    return pl.BlockSpec(memory_space=pltpu.HBM)


def smem():
    return pl.BlockSpec(memory_space=pltpu.SMEM)


def call(body, name, ins, outs, scratch=(), limit=24):
    return pl.pallas_call(
        body,
        name=name,
        in_specs=ins,
        out_shape=outs,
        out_specs=jax.tree.map(lambda _: vmem(), outs),
        scratch_shapes=scratch,
        compiler_params=pltpu.CompilerParams(vmem_limit_bytes=limit << 20),
    )


def shape(*dims, dtype=BF16):
    return jax.ShapeDtypeStruct(dims, dtype)


def iota(dims, axis):
    return lax.broadcasted_iota(jnp.int32, dims, axis)


def dot(a, b, dims=((1,), (0,))):
    return lax.dot_general(a, b, (dims, ((), ())), preferred_element_type=F32)


def row_order():
    to, source = iota((T, T), 0), iota((T, T), 1)
    return (source == (to % STEPS) * ROWS + to // STEPS).astype(F32).astype(BF16)


def rms(value, gain):
    return value * lax.rsqrt(jnp.mean(value * value, axis=1, keepdims=True) + EPS) * gain


def placed_rows(ids, gates, mixing):
    width = DESTS * SLOTS
    column = iota((T, width), 1)
    row = iota((T, width), 0)
    same_step = (row // ROWS) == (column // CAP) % STEPS
    below, above = iota((T, T), 0), iota((T, T), 1)
    earlier = ((below // ROWS == above // ROWS) & (above < below)).astype(F32).astype(BF16)
    order = row_order()
    ids = ids[0].reshape(T, TOP)
    gates = gates[0].reshape(T, TOP)
    shares = gates / jnp.sum(gates, axis=1, keepdims=True)
    named = jnp.zeros((T, width), F32)
    weight = jnp.zeros((T, width), F32)
    for k in range(TOP):
        match = (ids[:, k : k + 1] == column // SLOTS) & same_step
        named = jnp.where(match, 1.0, named)
        weight = jnp.where(match, shares[:, k : k + 1], weight)
    rank = dot(earlier, named.astype(BF16))
    keep = rank == (column % CAP).astype(F32)
    hit = jnp.where(keep, named, 0.0)
    share = jnp.where(keep, weight, 0.0)
    high = share.astype(BF16)
    low = (share - high.astype(F32)).astype(BF16)
    mixing[:T] = dot(order, high).astype(BF16)
    mixing[T:] = dot(order, low).astype(BF16)
    return dot(order, hit.astype(BF16)).astype(BF16)


def codec_body(books, table_mine, table_other, pieces):
    section = lax.axis_index("section")
    seq = lax.axis_index("seq")
    codes = table_mine.shape[0]
    line = iota((T, codes), 0)
    wanted = jnp.zeros((T, codes), jnp.int32)
    for row_at in range(ROWS):
        for step in range(STEPS):
            wanted = jnp.where(line == row_at * STEPS + step, books[step, row_at], wanted)
    found = jnp.zeros((T, D), F32)
    for owner, table in ((section, table_mine), (1 - section, table_other)):
        start = (owner * N_SEQ + seq) * codes
        picked = (wanted - start == iota((T, codes), 1)).astype(F32).astype(BF16)
        found = found + dot(picked, table[...])
    for s in range(0, N_SEQ, 2):
        rows_at = slice((s // 4) * ROWS, (s // 4 + 1) * ROWS)
        pair = [found[rows_at, (q % 4) * PIECE : (q % 4 + 1) * PIECE] for q in (s, s + 1)]
        pieces[s * ROWS : (s + 2) * ROWS] = jnp.concatenate(pair, axis=0).astype(BF16)


def lay_queries(hidden, gain, queries, values):
    normed = rms(hidden, gain)
    values[...] = hidden
    queries[...] = jnp.zeros_like(queries)
    for r in range(ROWS):
        for h in range(HEADS):
            k = h // GROUPS
            at = h * STEPS
            queries[r, at : at + STEPS, k * HEAD_DIM : (k + 1) * HEAD_DIM] = normed[
                r * STEPS : (r + 1) * STEPS, h * HEAD_DIM : (h + 1) * HEAD_DIM
            ]


def cache_copies(cache, kv, sems):
    half = ROWS // 2
    return [
        pltpu.make_async_copy(cache.at[0, r : r + half, i], kv.at[r : r + half, i], sems.at[r // half, i])
        for i in range(2)
        for r in range(0, ROWS, half)
    ]


def attend_rows(seq, lengths, kv, copies, queries, values, stats, scores, weights):
    lines = GROUPS * STEPS
    size = HEADS * STEPS
    ctx = scores.shape[1]
    lane = iota((STEPS, STAT), 1)
    step_of = iota((size, ctx), 0) % STEPS
    position = seq * ctx + iota((size, ctx), 1)
    for copy in copies[:2]:
        copy.wait()
    for r in range(ROWS):
        scores[r * size : (r + 1) * size] = dot(queries[r].astype(BF16), kv[r, 0], ((1,), (1,)))
    scales = []
    for r in range(ROWS):
        limit = jnp.where(step_of == 0, lengths[0, r], 0)
        for step in range(1, STEPS):
            limit = jnp.where(step_of == step, lengths[step, r], limit)
        live = position < limit
        score = jnp.where(live, scores[r * size : (r + 1) * size] * HEAD_DIM ** (-0.5), LOWEST)
        highest = jnp.max(score, axis=1, keepdims=True)
        weight = jnp.where(live, jnp.exp(score - highest), 0.0)
        total = jnp.sum(weight, axis=1, keepdims=True)
        some = total > 0.0
        safe = jnp.where(some, total, 1.0)
        log_sum = jnp.where(some, highest + jnp.log(safe), LOWEST)
        scales.append(1.0 / safe)
        weights[r * size : (r + 1) * size] = weight.astype(BF16)
        logs = jnp.broadcast_to(log_sum, (size, STAT))
        line_stats = jnp.zeros((STEPS, STAT), F32)
        for h in range(HEADS):
            line_stats = jnp.where(lane == h, logs[h * STEPS : (h + 1) * STEPS], line_stats)
        stats[r * STEPS : (r + 1) * STEPS, :] = line_stats
    for copy in copies[2:]:
        copy.wait()
    for r in range(ROWS):
        outs = dot(weights[r * size : (r + 1) * size], kv[r, 1])
        rows_at = slice(r * STEPS, (r + 1) * STEPS)
        for k in range(KV_HEADS):
            span = slice(k * lines, (k + 1) * lines)
            out = outs[span, k * HEAD_DIM : (k + 1) * HEAD_DIM] * scales[r][span]
            for g in range(GROUPS):
                h = k * GROUPS + g
                lanes_at = slice(h * HEAD_DIM, (h + 1) * HEAD_DIM)
                values[rows_at, lanes_at] = values[rows_at, lanes_at] + out[g * STEPS : (g + 1) * STEPS]


def spread_rows(values, stats, pick, sent):
    logs = stats[...]
    high = logs.astype(BF16).astype(F32)
    mid = (logs - high).astype(BF16).astype(F32)
    low = (logs - high - mid).astype(BF16).astype(F32)
    lane = iota((T, STAT), 1)
    packed = jnp.where(lane < 2 * HEADS, pltpu.roll(mid, HEADS, 1), pltpu.roll(low, 2 * HEADS, 1))
    packed = jnp.where(lane < HEADS, high, jnp.where(lane < 3 * HEADS, packed, 0.0))
    for at in range(0, D, 512):
        sent[:, at : at + 512] = dot(pick, values[:, at : at + 512].astype(BF16), ((0,), (0,))).astype(BF16)
    sent[:, D:] = dot(pick, packed.astype(BF16), ((0,), (0,))).astype(BF16)


def attend_body(
    layer, ids_in, gates_in, lengths_in, gains_in, cache, part_a, part_b,
    sent, mixing,
    ids, gates, lengths, gains, entry, kv, queries, values, stats, scores, weights, small_sems, sems,
):
    section = lax.axis_index("section")
    seq = lax.axis_index("seq")
    pairs = [(gains_in, gains), (ids_in, ids), (gates_in, gates), (lengths_in, lengths)]
    if layer == 0:
        pairs = [(part_a, entry)] + pairs
    small = [pltpu.make_async_copy(source, target, small_sems.at[i]) for i, (source, target) in enumerate(pairs)]
    copies = cache_copies(cache, kv, sems)
    for copy in small + copies:
        copy.start()
    for copy in small:
        copy.wait()
    if layer == 0:
        a = entry[...].astype(F32).reshape(T // 2, D)
        b = part_b[...].astype(F32).reshape(T // 2, D)
        rows = jnp.where(section == 0, jnp.concatenate([a, b], axis=0), jnp.concatenate([b, a], axis=0))
        hidden = dot(row_order(), rows.astype(BF16))
    else:
        codes = part_b[...].astype(F32)
        codes = jnp.concatenate(
            [
                jnp.concatenate([codes[s * ROWS : (s + 1) * ROWS] for s in range(b, b + 4)], axis=1)
                for b in range(0, N_SEQ, 4)
            ],
            axis=0,
        )
        hidden = part_a[...].astype(F32) + codes
    lay_queries(hidden, gains[0, 0:1, :], queries, values)
    pick = placed_rows(ids, gates, mixing)
    attend_rows(seq, lengths, kv, copies, queries, values, stats, scores, weights)
    spread_rows(values, stats, pick, sent)


def expert_body(got, gains_in, gate_in, up_in, down_in, sent, middle, gains, gate, up, down, sems):
    block = N_SEQ * SLOTS
    size = gate.shape[0] // CHUNKS
    pairs = [(gains_in, gains)]
    for j in range(CHUNKS):
        at = slice(j * size, (j + 1) * size)
        pairs += [(gate_in.at[0, 0, at], gate.at[at]), (up_in.at[0, 0, at], up.at[at])]
    for j in range(CHUNKS):
        at = slice(j * size, (j + 1) * size)
        pairs.append((down_in.at[0, 0, at], down.at[at]))
    copies = [pltpu.make_async_copy(source, target, sems.at[i]) for i, (source, target) in enumerate(pairs)]
    for copy in copies:
        copy.start()
    widen = (iota((STAT, D), 0) == iota((STAT, D), 1) // HEAD_DIM).astype(F32).astype(BF16)
    for x in range(N_EXPERT):
        rows_at = slice(x * block, (x + 1) * block)
        packed = got[rows_at, D:PAY].astype(F32)
        logs = packed + pltpu.roll(packed, STAT - HEADS, 1) + pltpu.roll(packed, STAT - 2 * HEADS, 1)
        logs = logs.reshape(N_SEQ, SLOTS, STAT)
        weights = jnp.exp(logs - jnp.max(logs, axis=0, keepdims=True))
        weights = weights / jnp.sum(weights, axis=0, keepdims=True)
        weights = weights.reshape(block, STAT)
        high = weights.astype(BF16)
        low = (weights - high.astype(F32)).astype(BF16)
        for at in range(0, D, 256):
            lanes_at = slice(at, at + 256)
            wide = dot(high, widen[:, lanes_at]) + dot(low, widen[:, lanes_at])
            part = (got[rows_at, lanes_at].astype(F32) * wide).reshape(N_SEQ, SLOTS, 256)
            middle[x * SLOTS : (x + 1) * SLOTS, lanes_at] = jnp.sum(part, axis=0)
    rows = middle[...]
    copies[0].wait()
    moe_in = rms(rows, gains[0, 1:2, :]).astype(BF16)
    activ = []
    for j in range(CHUNKS):
        at = slice(j * size, (j + 1) * size)
        copies[1 + 2 * j].wait()
        copies[2 + 2 * j].wait()
        gate_out = dot(moe_in, gate[at], ((1,), (1,)))
        up_out = dot(moe_in, up[at], ((1,), (1,)))
        activ.append((gate_out / (1.0 + jnp.exp(-gate_out)) * up_out).astype(BF16))
    total = jnp.zeros((T, D), F32)
    for j in range(CHUNKS):
        copies[1 + 2 * CHUNKS + j].wait()
        total = total + dot(activ[j], down[j * size : (j + 1) * size])
    result = total.astype(BF16).astype(F32) + rows
    for x in range(N_EXPERT):
        part = result[x * SLOTS : (x + 1) * SLOTS]
        pair = jnp.concatenate([part, part], axis=0).astype(BF16)
        for s in range(0, N_SEQ, 2):
            at = (x * N_SEQ + s) * SLOTS
            sent[at : at + 2 * SLOTS, :] = pair


def mix_body(got, mixing, out):
    both = dot(mixing[...], got[...])
    out[...] = (both[:T] + both[T:]).astype(BF16)


def head_body(mine, got, gain, table, out):
    last = lax.axis_index("section") == 1
    hidden = jnp.where(last, mine[...].astype(F32), got[...].astype(F32))
    final = rms(hidden, gain[...]).astype(BF16)
    final = dot(row_order(), final, ((0,), (0,))).astype(BF16)
    logits = dot(final, table[...], ((1,), (1,))) * D ** (-0.5)
    out[...] = logits.reshape(out.shape)


def in_hbm(value):
    return pltpu.with_memory_space_constraint(value, pltpu.HBM)


def swapped(value):
    return lax.ppermute(value, "section", [(0, 1), (1, 0)])


def exchanged(value):
    return lax.all_to_all(value, ("expert", "seq"), 0, 0, tiled=True)


def gathered(parts):
    held = lax.all_to_all(parts, "seq", 0, 0, tiled=True)
    held = jnp.sum(held.astype(F32).reshape(N_SEQ, ROWS, PIECE), axis=0).astype(BF16)
    return lax.all_to_all(jnp.tile(held, (N_SEQ, 1)), "seq", 0, 0, tiled=True)


def one_layer(layer, part_a, part_b, ids, gates, lengths, gains, cache, gate, up, down):
    _, _, _, ctx, kv_width = cache.shape
    lines = ROWS * HEADS * STEPS
    sent, mixing = call(
        functools.partial(attend_body, layer),
        "attend",
        [hbm()] * 5 + [vmem() if layer else hbm(), vmem()],
        (shape(DESTS * SLOTS, PAY), shape(2 * T, DESTS * SLOTS)),
        [
            pltpu.VMEM(ids.shape, jnp.int32),
            pltpu.VMEM(gates.shape, F32),
            pltpu.SMEM(lengths.shape, jnp.int32),
            pltpu.VMEM(gains.shape, F32),
            pltpu.VMEM((STEPS // 2, ROWS, D), BF16),
            pltpu.VMEM((ROWS, 2, ctx, kv_width), BF16),
            pltpu.VMEM((ROWS, HEADS * STEPS, kv_width), F32),
            pltpu.VMEM((T, D), F32),
            pltpu.VMEM((T, STAT), F32),
            pltpu.VMEM((lines, ctx), F32),
            pltpu.VMEM((lines, ctx), BF16),
            pltpu.SemaphoreType.DMA((5,)),
            pltpu.SemaphoreType.DMA((2, 2)),
        ],
    )(*(in_hbm(v) for v in (ids, gates, lengths, gains, cache)), part_a if layer else in_hbm(part_a), part_b)
    sent = call(
        expert_body,
        "experts",
        [vmem()] + [hbm()] * 4,
        shape(DESTS * SLOTS, D),
        [
            pltpu.VMEM((T, D), F32),
            pltpu.VMEM(gains.shape, F32),
            *(pltpu.VMEM(weight.shape[2:], BF16) for weight in (gate, up, down)),
            pltpu.SemaphoreType.DMA((1 + 3 * CHUNKS,)),
        ],
    )(exchanged(sent), *(in_hbm(v) for v in (gains, gate, up, down)))
    return call(mix_body, "mix", [vmem()] * 2, shape(T, D))(exchanged(sent), mixing)


def per_device(
    entry_rows,
    cache_entries,
    cache_lengths,
    norm_gains,
    expert_ids,
    gate_weights,
    gate_weight,
    up_weight,
    down_weight,
    codebook_ids,
    codec_table,
    final_gain,
):
    codes = codec_table.shape[0]
    section = lax.axis_index("section")
    held = (
        expert_ids,
        gate_weights,
        cache_lengths,
        norm_gains,
        cache_entries,
        gate_weight,
        up_weight,
        down_weight,
    )

    def first(entry, entry_got, books, table, table_got, *held):
        return one_layer(0, entry, entry_got, *held), jnp.zeros((N_SEQ * ROWS, PIECE), BF16)

    def codec(entry, entry_got, books, table, table_got, *held):
        pieces = call(codec_body, "codec", [smem()] + [vmem()] * 2, shape(N_SEQ * ROWS, PIECE))(
            books, table, table_got
        )
        return jnp.zeros((T, D), BF16), gathered(pieces)

    rows, pieces = lax.cond(
        section == 0,
        first,
        codec,
        entry_rows,
        swapped(entry_rows),
        codebook_ids,
        codec_table,
        swapped(codec_table),
        *held,
    )
    rows = lax.cond(
        section == 1,
        lambda *values: one_layer(1, *values),
        lambda *values: jnp.zeros((T, D), BF16),
        swapped(rows),
        pieces,
        *held,
    )
    rows_got = swapped(rows)
    return call(
        head_body,
        "head",
        [vmem()] * 4,
        shape(STEPS, ROWS, codes, dtype=F32),
    )(rows, rows_got, final_gain.reshape(1, D), codec_table)


def solution(mesh):
    placed = (
        P("section", "expert", None),
        P("section", "expert", None, "seq", None),
        P(None, "expert"),
        P("section", None, None),
        P("section", None, "expert", None),
        P("section", None, "expert", None),
        P("section", ("expert", "seq"), None, None),
        P("section", ("expert", "seq"), None, None),
        P("section", ("expert", "seq"), None, None),
        P(None, "expert"),
        P(("section", "seq"), None),
        P(),
    )
    return jax.shard_map(
        per_device,
        mesh=mesh,
        in_specs=placed,
        out_specs=P(None, "expert", ("section", "seq")),
        check_vma=False,
    )
```

```python
import functools

import jax
import jax.numpy as jnp
from jax import lax
from jax.experimental import pallas as pl
from jax.experimental.pallas import tpu as pltpu
from jax.sharding import PartitionSpec as P

F32 = jnp.float32
BF16 = jnp.bfloat16
STEPS = 4
ROWS = 8
D = 2048
HEAD_DIM = 128
HEADS = D // HEAD_DIM
KV_HEADS = 4
GROUPS = HEADS // KV_HEADS
TOP = 8
CAP = 2
N_EXPERT = 4
N_SEQ = 16
DESTS = N_EXPERT * N_SEQ
SLOTS = STEPS * CAP
T = STEPS * ROWS
STAT = 128
PAY = D + STAT
CHUNKS = 3
EPS = 1e-6
LOWEST = -1e30


def vmem():
    return pl.BlockSpec(memory_space=pltpu.VMEM)


def hbm():
    return pl.BlockSpec(memory_space=pltpu.HBM)


def smem():
    return pl.BlockSpec(memory_space=pltpu.SMEM)


def call(body, name, ins, outs, scratch=(), limit=24, places=None):
    return pl.pallas_call(
        body,
        name=name,
        in_specs=ins,
        out_shape=outs,
        out_specs=places or jax.tree.map(lambda _: vmem(), outs),
        scratch_shapes=scratch,
        compiler_params=pltpu.CompilerParams(vmem_limit_bytes=limit << 20),
    )


def shape(*dims, dtype=BF16):
    return jax.ShapeDtypeStruct(dims, dtype)


def iota(dims, axis):
    return lax.broadcasted_iota(jnp.int32, dims, axis)


def dot(a, b, dims=((1,), (0,))):
    return lax.dot_general(a, b, (dims, ((), ())), preferred_element_type=F32)


def row_order():
    to, source = iota((T, T), 0), iota((T, T), 1)
    return (source == (to % STEPS) * ROWS + to // STEPS).astype(F32).astype(BF16)


def rms(value, gain):
    return value * lax.rsqrt(jnp.mean(value * value, axis=1, keepdims=True) + EPS) * gain


def placed_rows(ids, gates, mixing):
    width = DESTS * SLOTS
    column = iota((T, width), 1)
    row = iota((T, width), 0)
    same_step = (row // ROWS) == (column // CAP) % STEPS
    below, above = iota((T, T), 0), iota((T, T), 1)
    earlier = ((below // ROWS == above // ROWS) & (above < below)).astype(F32).astype(BF16)
    order = row_order()
    ids = ids[0].reshape(T, TOP)
    gates = gates[0].reshape(T, TOP)
    shares = gates / jnp.sum(gates, axis=1, keepdims=True)
    named = jnp.zeros((T, width), F32)
    weight = jnp.zeros((T, width), F32)
    for k in range(TOP):
        match = (ids[:, k : k + 1] == column // SLOTS) & same_step
        named = jnp.where(match, 1.0, named)
        weight = jnp.where(match, shares[:, k : k + 1], weight)
    rank = dot(earlier, named.astype(BF16))
    keep = rank == (column % CAP).astype(F32)
    hit = jnp.where(keep, named, 0.0)
    share = jnp.where(keep, weight, 0.0)
    high = share.astype(BF16)
    low = (share - high.astype(F32)).astype(BF16)
    mixing[:T] = dot(order, high).astype(BF16)
    mixing[T:] = dot(order, low).astype(BF16)
    return dot(hit.astype(BF16), order, ((0,), (1,))).astype(BF16)


def codec_part(section, seq, books, tables):
    codes = tables[0].shape[0]
    line = iota((T, codes), 0)
    wanted = jnp.zeros((T, codes), jnp.int32)
    for row_at in range(ROWS):
        for step in range(STEPS):
            wanted = jnp.where(line == row_at * STEPS + step, books[step, row_at], wanted)
    found = jnp.zeros((T, D), F32)
    for owner, table in zip((section, 1 - section), tables):
        start = (owner * N_SEQ + seq) * codes
        picked = (wanted - start == iota((T, codes), 1)).astype(F32).astype(BF16)
        found = found + dot(picked, table[...])
    return found


def lay_queries(hidden, gain, queries, values):
    normed = rms(hidden, gain)
    values[...] = hidden
    queries[...] = jnp.zeros_like(queries)
    for r in range(ROWS):
        for h in range(HEADS):
            k = h // GROUPS
            at = h * STEPS
            queries[r, at : at + STEPS, k * HEAD_DIM : (k + 1) * HEAD_DIM] = normed[
                r * STEPS : (r + 1) * STEPS, h * HEAD_DIM : (h + 1) * HEAD_DIM
            ]


def cache_copies(cache, kv, sems):
    half = ROWS // 2
    return [
        pltpu.make_async_copy(cache.at[0, r : r + half, i], kv.at[r : r + half, i], sems.at[r // half, i])
        for i in range(2)
        for r in range(0, ROWS, half)
    ]


def softened(scores, live):
    score = jnp.where(live, scores * HEAD_DIM ** (-0.5), LOWEST)
    highest = jnp.max(score, axis=1, keepdims=True)
    weight = jnp.where(live, jnp.exp(score - highest), 0.0)
    total = jnp.sum(weight, axis=1, keepdims=True)
    some = total > 0.0
    safe = jnp.where(some, total, 1.0)
    return weight.astype(BF16), jnp.where(some, highest + jnp.log(safe), LOWEST), 1.0 / safe


def attend_rows(seq, lengths, kv, copies, queries, values, stats, scores, weights):
    lines = GROUPS * STEPS
    size = HEADS * STEPS
    ctx = scores.shape[1]
    lane = iota((STEPS, STAT), 1)
    step_of = iota((size, ctx), 0) % STEPS
    position = seq * ctx + iota((size, ctx), 1)
    for copy in copies[:2]:
        copy.wait()
    for r in range(ROWS):
        scores[r * size : (r + 1) * size] = dot(queries[r].astype(BF16), kv[r, 0], ((1,), (1,)))
    scales = []
    for r in range(ROWS):
        limit = jnp.where(step_of == 0, lengths[0, r], 0)
        for step in range(1, STEPS):
            limit = jnp.where(step_of == step, lengths[step, r], limit)
        weight, log_sum, scale = softened(scores[r * size : (r + 1) * size], position < limit)
        weights[r * size : (r + 1) * size] = weight
        scales.append(scale)
        logs = jnp.broadcast_to(log_sum, (size, STAT))
        line_stats = jnp.zeros((STEPS, STAT), F32)
        for h in range(HEADS):
            line_stats = jnp.where(lane == h, logs[h * STEPS : (h + 1) * STEPS], line_stats)
        stats[r * STEPS : (r + 1) * STEPS, :] = line_stats
    for copy in copies[2:]:
        copy.wait()
    for r in range(ROWS):
        outs = dot(weights[r * size : (r + 1) * size], kv[r, 1])
        rows_at = slice(r * STEPS, (r + 1) * STEPS)
        for k in range(KV_HEADS):
            span = slice(k * lines, (k + 1) * lines)
            out = outs[span, k * HEAD_DIM : (k + 1) * HEAD_DIM] * scales[r][span]
            for g in range(GROUPS):
                h = k * GROUPS + g
                lanes_at = slice(h * HEAD_DIM, (h + 1) * HEAD_DIM)
                values[rows_at, lanes_at] = values[rows_at, lanes_at] + out[g * STEPS : (g + 1) * STEPS]


def spread_rows(values, stats, pick, sent):
    width = values.shape[1]
    heads = width // HEAD_DIM
    logs = stats[...]
    high = logs.astype(BF16).astype(F32)
    mid = (logs - high).astype(BF16).astype(F32)
    low = (logs - high - mid).astype(BF16).astype(F32)
    lane = iota((T, STAT), 1)
    packed = jnp.where(lane < 2 * heads, pltpu.roll(mid, heads, 1), pltpu.roll(low, 2 * heads, 1))
    packed = jnp.where(lane < heads, high, jnp.where(lane < 3 * heads, packed, 0.0))
    for at in range(0, width, 512):
        sent[:, at : at + 512] = dot(pick, values[:, at : at + 512].astype(BF16)).astype(BF16)
    sent[:, width : width + STAT] = dot(pick, packed.astype(BF16)).astype(BF16)


def enter_body(
    ids_in, gates_in, lengths_in, gains_in, cache, entry_in, books_in, table_in, entry_got, table_got,
    sent, mixing, unused,
    ids, gates, lengths, gains, entry, books, table, kv, queries, values, stats, scores, weights, small_sems, sems,
):
    section = lax.axis_index("section")
    seq = lax.axis_index("seq")
    pairs = (
        (entry_in, entry),
        (gains_in, gains),
        (ids_in, ids),
        (gates_in, gates),
        (lengths_in, lengths),
        (books_in, books),
        (table_in, table),
    )
    small = [pltpu.make_async_copy(source, target, small_sems.at[i]) for i, (source, target) in enumerate(pairs)]
    copies = cache_copies(cache, kv, sems)
    for copy in small + copies:
        copy.start()
    for copy in small:
        copy.wait()
    a = entry[...].astype(F32).reshape(T // 2, D)
    b = entry_got[...].astype(F32).reshape(T // 2, D)
    rows = jnp.where(section == 0, jnp.concatenate([a, b], axis=0), jnp.concatenate([b, a], axis=0))
    lay_queries(dot(row_order(), rows.astype(BF16)), gains[0, 0:1, :], queries, values)
    pick = placed_rows(ids, gates, mixing)
    codes = codec_part(section, seq, books, (table, table_got))
    tiles = [
        codes[x * SLOTS : (x + 1) * SLOTS, s * STAT : (s + 1) * STAT] for x in range(N_EXPERT) for s in range(N_SEQ)
    ]
    sent[:, PAY:] = jnp.concatenate(tiles, axis=0).astype(BF16)
    attend_rows(seq, lengths, kv, copies, queries, values, stats, scores, weights)
    spread_rows(values, stats, pick, sent)


def trade_body(cache, out, held, parts, in_sems, out_sems):
    copies = [pltpu.make_async_copy(cache.at[0, r], held.at[r], in_sems.at[r]) for r in range(ROWS)]
    for copy in copies:
        copy.start()
    sends = []
    for r in range(ROWS):
        copies[r].wait()
        for k in range(KV_HEADS):
            parts[k, r] = held[r, :, :, k * HEAD_DIM : (k + 1) * HEAD_DIM]
    for k in range(KV_HEADS):
        sends.append(pltpu.make_async_copy(parts.at[k], out.at[k], out_sems.at[k]))
        sends[-1].start()
    for send in sends:
        send.wait()


def attend_body(
    ids_in, gates_in, lengths_in, gains_in, cache, rows,
    sent, mixing,
    ids, gates, lengths, gains, kv, normed, hidden, queries, values, stats, scores, weights, small_sems, sems,
):
    seq = lax.axis_index("seq")
    pairs = ((gains_in, gains), (ids_in, ids), (gates_in, gates), (lengths_in, lengths))
    small = [pltpu.make_async_copy(source, target, small_sems.at[i]) for i, (source, target) in enumerate(pairs)]
    local = cache.shape[3]
    copies = [
        pltpu.make_async_copy(cache.at[y, :, i], kv.at[:, i, y * local : (y + 1) * local], sems.at[i, y])
        for i in range(2)
        for y in range(KV_HEADS)
    ]
    for copy in small + copies:
        copy.start()
    whole = rows[...].astype(F32)
    hidden[...] = whole
    for copy in small:
        copy.wait()
    normed[...] = rms(whole, gains[0, 0:1, :])
    width = values.shape[1]
    own = pl.ds(pl.multiple_of((seq % KV_HEADS) * width, width), width)
    asked = normed[:, own]
    values[...] = hidden[:, own]
    size = GROUPS * STEPS
    for r in range(ROWS):
        for g in range(GROUPS):
            queries[r, g * STEPS : (g + 1) * STEPS, :] = asked[
                r * STEPS : (r + 1) * STEPS, g * HEAD_DIM : (g + 1) * HEAD_DIM
            ]
    pick = placed_rows(ids, gates, mixing)
    for copy in copies[:KV_HEADS]:
        copy.wait()
    for r in range(ROWS):
        scores[r * size : (r + 1) * size] = dot(queries[r].astype(BF16), kv[r, 0], ((1,), (1,)))
    ctx = scores.shape[1]
    step_of = iota((size, ctx), 0) % STEPS
    position = (seq // KV_HEADS) * ctx + iota((size, ctx), 1)
    lane = iota((STEPS, STAT), 1)
    scales = []
    for r in range(ROWS):
        limit = jnp.where(step_of == 0, lengths[0, r], 0)
        for step in range(1, STEPS):
            limit = jnp.where(step_of == step, lengths[step, r], limit)
        weight, log_sum, scale = softened(scores[r * size : (r + 1) * size], position < limit)
        weights[r * size : (r + 1) * size] = weight
        scales.append(scale)
        logs = jnp.broadcast_to(log_sum, (size, STAT))
        line_stats = jnp.zeros((STEPS, STAT), F32)
        for g in range(GROUPS):
            line_stats = jnp.where(lane == g, logs[g * STEPS : (g + 1) * STEPS], line_stats)
        stats[r * STEPS : (r + 1) * STEPS, :] = line_stats
    for copy in copies[KV_HEADS:]:
        copy.wait()
    for r in range(ROWS):
        out = dot(weights[r * size : (r + 1) * size], kv[r, 1]) * scales[r]
        rows_at = slice(r * STEPS, (r + 1) * STEPS)
        for g in range(GROUPS):
            lanes_at = slice(g * HEAD_DIM, (g + 1) * HEAD_DIM)
            values[rows_at, lanes_at] = values[rows_at, lanes_at] + out[g * STEPS : (g + 1) * STEPS]
    spread_rows(values, stats, pick, sent)


def expert_body(width, got, gains_in, gate_in, up_in, down_in, sent, middle, gains, gate, up, down, sems):
    block = N_SEQ * SLOTS
    size = gate.shape[0] // CHUNKS
    pairs = [(gains_in, gains)]
    for j in range(CHUNKS):
        at = slice(j * size, (j + 1) * size)
        pairs += [(gate_in.at[0, 0, at], gate.at[at]), (up_in.at[0, 0, at], up.at[at])]
    for j in range(CHUNKS):
        at = slice(j * size, (j + 1) * size)
        pairs.append((down_in.at[0, 0, at], down.at[at]))
    copies = [pltpu.make_async_copy(source, target, sems.at[i]) for i, (source, target) in enumerate(pairs)]
    for copy in copies:
        copy.start()
    heads = width // HEAD_DIM
    widen = (iota((2 * STAT, width), 0) % STAT == iota((2 * STAT, width), 1) // HEAD_DIM).astype(F32).astype(BF16)
    parts = D // width
    lines = parts * SLOTS
    for x in range(N_EXPERT):
        rows_at = slice(x * block, (x + 1) * block)
        packed = got[rows_at, width : width + STAT].astype(F32)
        logs = packed + pltpu.roll(packed, STAT - heads, 1) + pltpu.roll(packed, STAT - 2 * heads, 1)
        logs = logs.reshape(block // lines, lines, STAT)
        weights = jnp.exp(logs - jnp.max(logs, axis=0, keepdims=True))
        weights = weights / jnp.sum(weights, axis=0, keepdims=True)
        weights = weights.reshape(block, STAT)
        high = weights.astype(BF16)
        low = (weights - high.astype(F32)).astype(BF16)
        weights = jnp.concatenate([high, low], axis=1)
        for at in range(0, width, 256):
            lanes_at = slice(at, at + 256)
            wide = dot(weights, widen[:, lanes_at])
            part = (got[rows_at, lanes_at].astype(F32) * wide).reshape(block // lines, lines, 256)
            part = jnp.sum(part, axis=0)
            for y in range(parts):
                middle[x * SLOTS : (x + 1) * SLOTS, y * width + at : y * width + at + 256] = part[
                    y * SLOTS : (y + 1) * SLOTS
                ]
    rows = middle[...]
    copies[0].wait()
    moe_in = rms(rows, gains[0, 1:2, :]).astype(BF16)
    activ = []
    for j in range(CHUNKS):
        at = slice(j * size, (j + 1) * size)
        copies[1 + 2 * j].wait()
        copies[2 + 2 * j].wait()
        gate_out = dot(moe_in, gate[at], ((1,), (1,)))
        up_out = dot(moe_in, up[at], ((1,), (1,)))
        activ.append((gate_out / (1.0 + jnp.exp(-gate_out)) * up_out).astype(BF16))
    total = jnp.zeros((T, D), F32)
    for j in range(CHUNKS):
        copies[1 + 2 * CHUNKS + j].wait()
        total = total + dot(activ[j], down[j * size : (j + 1) * size])
    result = total.astype(BF16).astype(F32) + rows
    coded = got.shape[1] > width + STAT
    if coded:
        codes = jnp.sum(got[:, width + STAT :].astype(F32).reshape(N_EXPERT, N_SEQ, SLOTS, STAT), axis=1)
    for x in range(N_EXPERT):
        part = result[x * SLOTS : (x + 1) * SLOTS]
        if coded:
            part = jnp.concatenate([part, codes[x]], axis=1)
        pair = jnp.concatenate([part, part], axis=0).astype(BF16)
        for s in range(0, N_SEQ, 2):
            at = (x * N_SEQ + s) * SLOTS
            sent[at : at + 2 * SLOTS, :] = pair


def mix_body(got, mixing, out):
    both = dot(mixing[...], got[:, :D])
    hidden = (both[:T] + both[T:]).astype(BF16)
    if got.shape[1] > D:
        codes = got[:, D:].astype(F32)
        lines = [
            jnp.concatenate(
                [codes[(x * N_SEQ + s) * SLOTS : (x * N_SEQ + s + 1) * SLOTS] for s in range(N_SEQ)], axis=1
            )
            for x in range(N_EXPERT)
        ]
        hidden = hidden.astype(F32) + jnp.concatenate(lines, axis=0)
    out[...] = hidden.astype(out.dtype)


def head_body(mine, got, gain, table, out):
    last = lax.axis_index("section") == 1
    hidden = jnp.where(last, mine[...].astype(F32), got[...].astype(F32))
    final = rms(hidden, gain[...]).astype(BF16)
    final = dot(row_order(), final, ((0,), (0,))).astype(BF16)
    logits = dot(final, table[...], ((1,), (1,))) * D ** (-0.5)
    out[...] = logits.reshape(out.shape)


def in_hbm(value):
    return pltpu.with_memory_space_constraint(value, pltpu.HBM)


def swapped(value):
    return lax.ppermute(value, "section", [(0, 1), (1, 0)])


def exchanged(value):
    return lax.all_to_all(value, ("expert", "seq"), 0, 0, tiled=True)


def traded(cache):
    _, rows, kinds, ctx, _ = cache.shape
    parts = pl.pallas_call(
        trade_body,
        name="trade",
        in_specs=[hbm()],
        out_specs=hbm(),
        out_shape=shape(KV_HEADS, rows, kinds, ctx, HEAD_DIM),
        scratch_shapes=[
            pltpu.VMEM(cache.shape[1:], BF16),
            pltpu.VMEM((KV_HEADS, rows, kinds, ctx, HEAD_DIM), BF16),
            pltpu.SemaphoreType.DMA((rows,)),
            pltpu.SemaphoreType.DMA((KV_HEADS,)),
        ],
        compiler_params=pltpu.CompilerParams(vmem_limit_bytes=56 << 20),
    )(in_hbm(cache))
    groups = [list(range(at, at + KV_HEADS)) for at in range(0, N_SEQ, KV_HEADS)]
    return lax.all_to_all(parts, "seq", 0, 0, axis_index_groups=groups, tiled=True)


def experts(width, sent, mixing, gains, gate, up, down):
    coded = STAT if sent.shape[1] > width + STAT else 0
    sent = call(
        functools.partial(expert_body, width),
        "experts",
        [vmem()] + [hbm()] * 4,
        shape(DESTS * SLOTS, D + coded),
        [
            pltpu.VMEM((T, D), F32),
            pltpu.VMEM(gains.shape, F32),
            *(pltpu.VMEM(weight.shape[2:], BF16) for weight in (gate, up, down)),
            pltpu.SemaphoreType.DMA((1 + 3 * CHUNKS,)),
        ],
    )(exchanged(sent), *(in_hbm(v) for v in (gains, gate, up, down)))
    return call(mix_body, "mix", [vmem()] * 2, shape(T, D))(exchanged(sent), mixing)


def per_device(
    entry_rows,
    cache_entries,
    cache_lengths,
    norm_gains,
    expert_ids,
    gate_weights,
    gate_weight,
    up_weight,
    down_weight,
    codebook_ids,
    codec_table,
    final_gain,
):
    codes = codec_table.shape[0]
    section = lax.axis_index("section")
    ctx = cache_entries.shape[3]
    kv_width = cache_entries.shape[4]
    width = DESTS * SLOTS

    def small(ids, gates, lengths, gains, *rest):
        return [
            pltpu.VMEM(ids.shape, jnp.int32),
            pltpu.VMEM(gates.shape, F32),
            pltpu.SMEM(lengths.shape, jnp.int32),
            pltpu.VMEM(gains.shape, F32),
        ]

    def first(entry, entry_got, books, table, table_got, cache, weights, *held):
        lines = ROWS * HEADS * STEPS
        sent, mixing, unused = call(
            enter_body,
            "enter",
            [hbm()] * 8 + [vmem()] * 2,
            (shape(width, PAY + STAT), shape(2 * T, width), shape(KV_HEADS, ROWS, 2, ctx, HEAD_DIM)),
            [
                *small(*held),
                pltpu.VMEM(entry.shape, BF16),
                pltpu.SMEM(books.shape, jnp.int32),
                pltpu.VMEM(table.shape, BF16),
                pltpu.VMEM((ROWS, 2, ctx, kv_width), BF16),
                pltpu.VMEM((ROWS, HEADS * STEPS, kv_width), F32),
                pltpu.VMEM((T, D), F32),
                pltpu.VMEM((T, STAT), F32),
                pltpu.VMEM((lines, ctx), F32),
                pltpu.VMEM((lines, ctx), BF16),
                pltpu.SemaphoreType.DMA((7,)),
                pltpu.SemaphoreType.DMA((2, 2)),
            ],
            places=(vmem(), vmem(), hbm()),
        )(*(in_hbm(v) for v in (*held, cache, entry, books, table)), entry_got, table_got)
        return experts(D, sent, mixing, held[3], *weights), unused

    def waiting(entry, entry_got, books, table, table_got, cache, weights, *held):
        return jnp.zeros((T, D), BF16), traded(cache)

    def second(rows, cache, weights, *held):
        lines = ROWS * GROUPS * STEPS
        span = KV_HEADS * ctx
        share = GROUPS * HEAD_DIM
        sent, mixing = call(
            attend_body,
            "attend",
            [hbm()] * 5 + [vmem()],
            (shape(width, share + STAT), shape(2 * T, width)),
            [
                *small(*held),
                pltpu.VMEM((ROWS, 2, span, HEAD_DIM), BF16),
                pltpu.VMEM((T, D), F32),
                pltpu.VMEM((T, D), F32),
                pltpu.VMEM((ROWS, GROUPS * STEPS, HEAD_DIM), F32),
                pltpu.VMEM((T, share), F32),
                pltpu.VMEM((T, STAT), F32),
                pltpu.VMEM((lines, span), F32),
                pltpu.VMEM((lines, span), BF16),
                pltpu.SemaphoreType.DMA((4,)),
                pltpu.SemaphoreType.DMA((2, KV_HEADS)),
            ],
        )(*(in_hbm(v) for v in (*held, cache)), rows)
        return experts(share, sent, mixing, held[3], *weights)

    held = (expert_ids, gate_weights, cache_lengths, norm_gains)
    weights = (gate_weight, up_weight, down_weight)
    rows, cache = lax.cond(
        section == 0,
        first,
        waiting,
        entry_rows,
        swapped(entry_rows),
        codebook_ids,
        codec_table,
        swapped(codec_table),
        cache_entries,
        weights,
        *held,
    )
    rows = lax.cond(
        section == 1,
        second,
        lambda *values: jnp.zeros((T, D), BF16),
        swapped(rows),
        cache,
        weights,
        *held,
    )
    rows_got = swapped(rows)
    return call(
        head_body,
        "head",
        [vmem()] * 4,
        shape(STEPS, ROWS, codes, dtype=F32),
    )(rows, rows_got, final_gain.reshape(1, D), codec_table)


def solution(mesh):
    placed = (
        P("section", "expert", None),
        P("section", "expert", None, "seq", None),
        P(None, "expert"),
        P("section", None, None),
        P("section", None, "expert", None),
        P("section", None, "expert", None),
        P("section", ("expert", "seq"), None, None),
        P("section", ("expert", "seq"), None, None),
        P("section", ("expert", "seq"), None, None),
        P(None, "expert"),
        P(("section", "seq"), None),
        P(),
    )
    return jax.shard_map(
        per_device,
        mesh=mesh,
        in_specs=placed,
        out_specs=P(None, "expert", ("section", "seq")),
        check_vma=False,
    )
```

```python
import functools

import jax
import jax.numpy as jnp
from jax import lax
from jax.experimental import pallas as pl
from jax.experimental.pallas import tpu as pltpu
from jax.sharding import PartitionSpec as P

F32 = jnp.float32
BF16 = jnp.bfloat16
STEPS = 4
ROWS = 8
D = 2048
HEAD_DIM = 128
HEADS = D // HEAD_DIM
KV_HEADS = 4
GROUPS = HEADS // KV_HEADS
TOP = 8
CAP = 2
N_EXPERT = 4
N_SEQ = 16
DESTS = N_EXPERT * N_SEQ
SLOTS = STEPS * CAP
T = STEPS * ROWS
STAT = 128
PAY = D + STAT
CHUNKS = 3
EPS = 1e-6
LOWEST = -1e30


def vmem():
    return pl.BlockSpec(memory_space=pltpu.VMEM)


def hbm():
    return pl.BlockSpec(memory_space=pltpu.HBM)


def smem():
    return pl.BlockSpec(memory_space=pltpu.SMEM)


def call(body, name, ins, outs, scratch=(), limit=24, places=None):
    return pl.pallas_call(
        body,
        name=name,
        in_specs=ins,
        out_shape=outs,
        out_specs=places or jax.tree.map(lambda _: vmem(), outs),
        scratch_shapes=scratch,
        compiler_params=pltpu.CompilerParams(vmem_limit_bytes=limit << 20),
    )


def shape(*dims, dtype=BF16):
    return jax.ShapeDtypeStruct(dims, dtype)


def iota(dims, axis):
    return lax.broadcasted_iota(jnp.int32, dims, axis)


def dot(a, b, dims=((1,), (0,))):
    return lax.dot_general(a, b, (dims, ((), ())), preferred_element_type=F32)


def row_order():
    to, source = iota((T, T), 0), iota((T, T), 1)
    return (source == (to % STEPS) * ROWS + to // STEPS).astype(F32).astype(BF16)


def rms(value, gain):
    return value * lax.rsqrt(jnp.mean(value * value, axis=1, keepdims=True) + EPS) * gain


def named_slots(ids, gates=None):
    width = DESTS * SLOTS
    column = iota((T, width), 1)
    row = iota((T, width), 0)
    same_step = (row // ROWS) == (column // CAP) % STEPS
    below, above = iota((T, T), 0), iota((T, T), 1)
    earlier = ((below // ROWS == above // ROWS) & (above < below)).astype(F32).astype(BF16)
    ids = ids[0].reshape(T, TOP)
    named = jnp.zeros((T, width), F32)
    weight = jnp.zeros((T, width), F32)
    if gates is not None:
        gates = gates[0].reshape(T, TOP)
        shares = gates / jnp.sum(gates, axis=1, keepdims=True)
    for k in range(TOP):
        match = (ids[:, k : k + 1] == column // SLOTS) & same_step
        named = jnp.where(match, 1.0, named)
        if gates is not None:
            weight = jnp.where(match, shares[:, k : k + 1], weight)
    keep = dot(earlier, named.astype(BF16)) == (column % CAP).astype(F32)
    return jnp.where(keep, named if gates is None else weight, 0.0)


def slot_rows(ids):
    return dot(named_slots(ids).astype(BF16), row_order(), ((0,), (1,))).astype(BF16)


def mix_rows(ids, gates, mixing):
    share = named_slots(ids, gates)
    high = share.astype(BF16)
    low = (share - high.astype(F32)).astype(BF16)
    mixing[:T] = dot(row_order(), high).astype(BF16)
    mixing[T:] = dot(row_order(), low).astype(BF16)


def codec_part(section, seq, books, tables):
    codes = tables[0].shape[0]
    line = iota((T, codes), 0)
    wanted = jnp.zeros((T, codes), jnp.int32)
    for row_at in range(ROWS):
        for step in range(STEPS):
            wanted = jnp.where(line == row_at * STEPS + step, books[step, row_at], wanted)
    found = jnp.zeros((T, D), F32)
    for owner, table in zip((section, 1 - section), tables):
        start = (owner * N_SEQ + seq) * codes
        picked = (wanted - start == iota((T, codes), 1)).astype(F32).astype(BF16)
        found = found + dot(picked, table[...])
    return found


def lay_queries(hidden, gain, queries, values):
    normed = rms(hidden, gain)
    values[...] = hidden
    queries[...] = jnp.zeros_like(queries)
    for r in range(ROWS):
        for h in range(HEADS):
            k = h // GROUPS
            at = h * STEPS
            queries[r, at : at + STEPS, k * HEAD_DIM : (k + 1) * HEAD_DIM] = normed[
                r * STEPS : (r + 1) * STEPS, h * HEAD_DIM : (h + 1) * HEAD_DIM
            ]


def cache_copies(cache, kv, sems):
    half = ROWS // 2
    return [
        pltpu.make_async_copy(cache.at[0, r : r + half, i], kv.at[r : r + half, i], sems.at[r // half, i])
        for i in range(2)
        for r in range(0, ROWS, half)
    ]


def softened(scores, live):
    score = jnp.where(live, scores * HEAD_DIM ** (-0.5), LOWEST)
    highest = jnp.max(score, axis=1, keepdims=True)
    weight = jnp.where(live, jnp.exp(score - highest), 0.0)
    total = jnp.sum(weight, axis=1, keepdims=True)
    some = total > 0.0
    safe = jnp.where(some, total, 1.0)
    return weight.astype(BF16), jnp.where(some, highest + jnp.log(safe), LOWEST), 1.0 / safe


def attend_rows(seq, lengths, kv, copies, queries, values, stats, scores, weights):
    lines = GROUPS * STEPS
    size = HEADS * STEPS
    ctx = scores.shape[1]
    lane = iota((STEPS, STAT), 1)
    step_of = iota((size, ctx), 0) % STEPS
    position = seq * ctx + iota((size, ctx), 1)
    for copy in copies[:2]:
        copy.wait()
    for r in range(ROWS):
        scores[r * size : (r + 1) * size] = dot(queries[r].astype(BF16), kv[r, 0], ((1,), (1,)))
    scales = []
    for r in range(ROWS):
        limit = jnp.where(step_of == 0, lengths[0, r], 0)
        for step in range(1, STEPS):
            limit = jnp.where(step_of == step, lengths[step, r], limit)
        weight, log_sum, scale = softened(scores[r * size : (r + 1) * size], position < limit)
        weights[r * size : (r + 1) * size] = weight
        scales.append(scale)
        logs = jnp.broadcast_to(log_sum, (size, STAT))
        line_stats = jnp.zeros((STEPS, STAT), F32)
        for h in range(HEADS):
            line_stats = jnp.where(lane == h, logs[h * STEPS : (h + 1) * STEPS], line_stats)
        stats[r * STEPS : (r + 1) * STEPS, :] = line_stats
    for copy in copies[2:]:
        copy.wait()
    for r in range(ROWS):
        outs = dot(weights[r * size : (r + 1) * size], kv[r, 1])
        rows_at = slice(r * STEPS, (r + 1) * STEPS)
        for k in range(KV_HEADS):
            span = slice(k * lines, (k + 1) * lines)
            out = outs[span, k * HEAD_DIM : (k + 1) * HEAD_DIM] * scales[r][span]
            for g in range(GROUPS):
                h = k * GROUPS + g
                lanes_at = slice(h * HEAD_DIM, (h + 1) * HEAD_DIM)
                values[rows_at, lanes_at] = values[rows_at, lanes_at] + out[g * STEPS : (g + 1) * STEPS]


def spread_rows(values, stats, pick, sent):
    width = values.shape[1]
    heads = width // HEAD_DIM
    logs = stats[...]
    high = logs.astype(BF16).astype(F32)
    mid = (logs - high).astype(BF16).astype(F32)
    low = (logs - high - mid).astype(BF16).astype(F32)
    lane = iota((T, STAT), 1)
    packed = jnp.where(lane < 2 * heads, pltpu.roll(mid, heads, 1), pltpu.roll(low, 2 * heads, 1))
    packed = jnp.where(lane < heads, high, jnp.where(lane < 3 * heads, packed, 0.0))
    for at in range(0, width, 512):
        sent[:, at : at + 512] = dot(pick, values[:, at : at + 512].astype(BF16)).astype(BF16)
    sent[:, width : width + STAT] = dot(pick, packed.astype(BF16)).astype(BF16)


def enter_body(
    ids_in, lengths_in, gains_in, cache, entry_in, books_in, table_in, gate_in, entry_got, table_got,
    sent, gate, unused,
    ids, lengths, gains, entry, books, table, kv, queries, values, stats, scores, weights, small_sems, sems, ahead_sem,
):
    section = lax.axis_index("section")
    seq = lax.axis_index("seq")
    pairs = (
        (entry_in, entry),
        (gains_in, gains),
        (ids_in, ids),
        (lengths_in, lengths),
        (books_in, books),
        (table_in, table),
    )
    small = [pltpu.make_async_copy(source, target, small_sems.at[i]) for i, (source, target) in enumerate(pairs)]
    copies = cache_copies(cache, kv, sems)
    ahead = pltpu.make_async_copy(gate_in.at[0, 0], gate, ahead_sem.at[0])
    for copy in [*small, *copies, ahead]:
        copy.start()
    for copy in small:
        copy.wait()
    a = entry[...].astype(F32).reshape(T // 2, D)
    b = entry_got[...].astype(F32).reshape(T // 2, D)
    rows = jnp.where(section == 0, jnp.concatenate([a, b], axis=0), jnp.concatenate([b, a], axis=0))
    lay_queries(dot(row_order(), rows.astype(BF16)), gains[0, 0:1, :], queries, values)
    pick = slot_rows(ids)
    codes = codec_part(section, seq, books, (table, table_got))
    tiles = [
        codes[x * SLOTS : (x + 1) * SLOTS, s * STAT : (s + 1) * STAT] for x in range(N_EXPERT) for s in range(N_SEQ)
    ]
    sent[:, PAY:] = jnp.concatenate(tiles, axis=0).astype(BF16)
    attend_rows(seq, lengths, kv, copies, queries, values, stats, scores, weights)
    spread_rows(values, stats, pick, sent)
    ahead.wait()


def trade_body(cache, out, held, parts, in_sems, out_sems):
    copies = [pltpu.make_async_copy(cache.at[0, r], held.at[r], in_sems.at[r]) for r in range(ROWS)]
    for copy in copies:
        copy.start()
    sends = []
    for r in range(ROWS):
        copies[r].wait()
        for k in range(KV_HEADS):
            parts[k, r] = held[r, :, :, k * HEAD_DIM : (k + 1) * HEAD_DIM]
    for k in range(KV_HEADS):
        sends.append(pltpu.make_async_copy(parts.at[k], out.at[k], out_sems.at[k]))
        sends[-1].start()
    for send in sends:
        send.wait()


def attend_body(
    ids_in, lengths_in, gains_in, cache, gate_in, rows,
    sent, gate,
    ids, lengths, gains, kv, normed, hidden, queries, values, stats, scores, weights, small_sems, sems, ahead_sem,
):
    seq = lax.axis_index("seq")
    pairs = ((gains_in, gains), (ids_in, ids), (lengths_in, lengths))
    small = [pltpu.make_async_copy(source, target, small_sems.at[i]) for i, (source, target) in enumerate(pairs)]
    local = cache.shape[3]
    copies = [
        pltpu.make_async_copy(cache.at[y, :, i], kv.at[:, i, y * local : (y + 1) * local], sems.at[i, y])
        for i in range(2)
        for y in range(KV_HEADS)
    ]
    ahead = pltpu.make_async_copy(gate_in.at[0, 0], gate, ahead_sem.at[0])
    for copy in [*small, *copies, ahead]:
        copy.start()
    whole = rows[...].astype(F32)
    hidden[...] = whole
    for copy in small:
        copy.wait()
    normed[...] = rms(whole, gains[0, 0:1, :])
    width = values.shape[1]
    own = pl.ds(pl.multiple_of((seq % KV_HEADS) * width, width), width)
    asked = normed[:, own]
    values[...] = hidden[:, own]
    size = GROUPS * STEPS
    for r in range(ROWS):
        for g in range(GROUPS):
            queries[r, g * STEPS : (g + 1) * STEPS, :] = asked[
                r * STEPS : (r + 1) * STEPS, g * HEAD_DIM : (g + 1) * HEAD_DIM
            ]
    pick = slot_rows(ids)
    for copy in copies[:KV_HEADS]:
        copy.wait()
    for r in range(ROWS):
        scores[r * size : (r + 1) * size] = dot(queries[r].astype(BF16), kv[r, 0], ((1,), (1,)))
    ctx = scores.shape[1]
    step_of = iota((size, ctx), 0) % STEPS
    position = (seq // KV_HEADS) * ctx + iota((size, ctx), 1)
    lane = iota((STEPS, STAT), 1)
    scales = []
    for r in range(ROWS):
        limit = jnp.where(step_of == 0, lengths[0, r], 0)
        for step in range(1, STEPS):
            limit = jnp.where(step_of == step, lengths[step, r], limit)
        weight, log_sum, scale = softened(scores[r * size : (r + 1) * size], position < limit)
        weights[r * size : (r + 1) * size] = weight
        scales.append(scale)
        logs = jnp.broadcast_to(log_sum, (size, STAT))
        line_stats = jnp.zeros((STEPS, STAT), F32)
        for g in range(GROUPS):
            line_stats = jnp.where(lane == g, logs[g * STEPS : (g + 1) * STEPS], line_stats)
        stats[r * STEPS : (r + 1) * STEPS, :] = line_stats
    for copy in copies[KV_HEADS:]:
        copy.wait()
    for r in range(ROWS):
        out = dot(weights[r * size : (r + 1) * size], kv[r, 1]) * scales[r]
        rows_at = slice(r * STEPS, (r + 1) * STEPS)
        for g in range(GROUPS):
            lanes_at = slice(g * HEAD_DIM, (g + 1) * HEAD_DIM)
            values[rows_at, lanes_at] = values[rows_at, lanes_at] + out[g * STEPS : (g + 1) * STEPS]
    spread_rows(values, stats, pick, sent)
    ahead.wait()


def expert_body(
    width, got, ids_in, gates_in, gains_in, gate, up_in, down_in,
    sent, mixing,
    middle, ids, gates, gains, up, down, sems,
):
    block = N_SEQ * SLOTS
    size = gate.shape[0] // CHUNKS
    pairs = [(gains_in, gains), (ids_in, ids), (gates_in, gates)]
    for source, target in ((up_in, up), (down_in, down)):
        for j in range(0, CHUNKS * size, size):
            pairs.append((source.at[0, 0, j : j + size], target.at[j : j + size]))
    copies = [pltpu.make_async_copy(source, target, sems.at[i]) for i, (source, target) in enumerate(pairs)]
    for copy in copies:
        copy.start()
    heads = width // HEAD_DIM
    widen = (iota((2 * STAT, width), 0) % STAT == iota((2 * STAT, width), 1) // HEAD_DIM).astype(F32).astype(BF16)
    parts = D // width
    lines = parts * SLOTS
    for x in range(N_EXPERT):
        rows_at = slice(x * block, (x + 1) * block)
        packed = got[rows_at, width : width + STAT].astype(F32)
        logs = packed + pltpu.roll(packed, STAT - heads, 1) + pltpu.roll(packed, STAT - 2 * heads, 1)
        logs = logs.reshape(block // lines, lines, STAT)
        weights = jnp.exp(logs - jnp.max(logs, axis=0, keepdims=True))
        weights = weights / jnp.sum(weights, axis=0, keepdims=True)
        weights = weights.reshape(block, STAT)
        high = weights.astype(BF16)
        low = (weights - high.astype(F32)).astype(BF16)
        weights = jnp.concatenate([high, low], axis=1)
        for at in range(0, width, 256):
            lanes_at = slice(at, at + 256)
            wide = dot(weights, widen[:, lanes_at])
            part = (got[rows_at, lanes_at].astype(F32) * wide).reshape(block // lines, lines, 256)
            part = jnp.sum(part, axis=0)
            for y in range(parts):
                middle[x * SLOTS : (x + 1) * SLOTS, y * width + at : y * width + at + 256] = part[
                    y * SLOTS : (y + 1) * SLOTS
                ]
    rows = middle[...]
    for copy in copies[:3]:
        copy.wait()
    mix_rows(ids, gates, mixing)
    moe_in = rms(rows, gains[0, 1:2, :]).astype(BF16)
    activ = []
    for j in range(CHUNKS):
        at = slice(j * size, (j + 1) * size)
        copies[3 + j].wait()
        gate_out = dot(moe_in, gate[at], ((1,), (1,)))
        up_out = dot(moe_in, up[at], ((1,), (1,)))
        activ.append((gate_out / (1.0 + jnp.exp(-gate_out)) * up_out).astype(BF16))
    total = jnp.zeros((T, D), F32)
    for j in range(CHUNKS):
        copies[3 + CHUNKS + j].wait()
        total = total + dot(activ[j], down[j * size : (j + 1) * size])
    result = total.astype(BF16).astype(F32) + rows
    coded = got.shape[1] > width + STAT
    if coded:
        codes = jnp.sum(got[:, width + STAT :].astype(F32).reshape(N_EXPERT, N_SEQ, SLOTS, STAT), axis=1)
    for x in range(N_EXPERT):
        part = result[x * SLOTS : (x + 1) * SLOTS]
        if coded:
            part = jnp.concatenate([part, codes[x]], axis=1)
        pair = jnp.concatenate([part, part], axis=0).astype(BF16)
        for s in range(0, N_SEQ, 2):
            at = (x * N_SEQ + s) * SLOTS
            sent[at : at + 2 * SLOTS, :] = pair


def mix_body(got, mixing, out):
    both = dot(mixing[...], got[:, :D])
    hidden = (both[:T] + both[T:]).astype(BF16)
    if got.shape[1] > D:
        codes = got[:, D:].astype(F32)
        lines = [
            jnp.concatenate(
                [codes[(x * N_SEQ + s) * SLOTS : (x * N_SEQ + s + 1) * SLOTS] for s in range(N_SEQ)], axis=1
            )
            for x in range(N_EXPERT)
        ]
        hidden = hidden.astype(F32) + jnp.concatenate(lines, axis=0)
    out[...] = hidden.astype(out.dtype)


def head_body(mine, got, gain, table, out):
    last = lax.axis_index("section") == 1
    hidden = jnp.where(last, mine[...].astype(F32), got[...].astype(F32))
    final = rms(hidden, gain[...]).astype(BF16)
    final = dot(row_order(), final, ((0,), (0,))).astype(BF16)
    logits = dot(final, table[...], ((1,), (1,))) * D ** (-0.5)
    out[...] = logits.reshape(out.shape)


def in_hbm(value):
    return pltpu.with_memory_space_constraint(value, pltpu.HBM)


def swapped(value):
    return lax.ppermute(value, "section", [(0, 1), (1, 0)])


def exchanged(value):
    return lax.all_to_all(value, ("expert", "seq"), 0, 0, tiled=True)


def traded(cache):
    _, rows, kinds, ctx, _ = cache.shape
    parts = pl.pallas_call(
        trade_body,
        name="trade",
        in_specs=[hbm()],
        out_specs=hbm(),
        out_shape=shape(KV_HEADS, rows, kinds, ctx, HEAD_DIM),
        scratch_shapes=[
            pltpu.VMEM(cache.shape[1:], BF16),
            pltpu.VMEM((KV_HEADS, rows, kinds, ctx, HEAD_DIM), BF16),
            pltpu.SemaphoreType.DMA((rows,)),
            pltpu.SemaphoreType.DMA((KV_HEADS,)),
        ],
        compiler_params=pltpu.CompilerParams(vmem_limit_bytes=56 << 20),
    )(in_hbm(cache))
    groups = [list(range(at, at + KV_HEADS)) for at in range(0, N_SEQ, KV_HEADS)]
    return lax.all_to_all(parts, "seq", 0, 0, axis_index_groups=groups, tiled=True)


def experts(width, sent, ids, gates, gains, gate, up, down):
    coded = STAT if sent.shape[1] > width + STAT else 0
    sent, mixing = call(
        functools.partial(expert_body, width),
        "experts",
        [vmem()] + [hbm()] * 3 + [vmem()] + [hbm()] * 2,
        (shape(DESTS * SLOTS, D + coded), shape(2 * T, DESTS * SLOTS)),
        [
            pltpu.VMEM((T, D), F32),
            pltpu.VMEM(ids.shape, jnp.int32),
            pltpu.VMEM(gates.shape, F32),
            pltpu.VMEM(gains.shape, F32),
            *(pltpu.VMEM(weight.shape[2:], BF16) for weight in (up, down)),
            pltpu.SemaphoreType.DMA((3 + 2 * CHUNKS,)),
        ],
    )(exchanged(sent), in_hbm(ids), in_hbm(gates), in_hbm(gains), gate, in_hbm(up), in_hbm(down))
    return call(mix_body, "mix", [vmem()] * 2, shape(T, D))(exchanged(sent), mixing)


def per_device(
    entry_rows,
    cache_entries,
    cache_lengths,
    norm_gains,
    expert_ids,
    gate_weights,
    gate_weight,
    up_weight,
    down_weight,
    codebook_ids,
    codec_table,
    final_gain,
):
    codes = codec_table.shape[0]
    section = lax.axis_index("section")
    ctx = cache_entries.shape[3]
    kv_width = cache_entries.shape[4]
    width = DESTS * SLOTS

    def small(ids, lengths, gains):
        return [
            pltpu.VMEM(ids.shape, jnp.int32),
            pltpu.SMEM(lengths.shape, jnp.int32),
            pltpu.VMEM(gains.shape, F32),
        ]

    def first(entry, entry_got, books, table, table_got, cache, weights, *held):
        lines = ROWS * HEADS * STEPS
        sent, gate, unused = call(
            enter_body,
            "enter",
            [hbm()] * 8 + [vmem()] * 2,
            (shape(width, PAY + STAT), shape(*gate_weight.shape[2:]), shape(KV_HEADS, ROWS, 2, ctx, HEAD_DIM)),
            [
                *small(held[0], *held[2:]),
                pltpu.VMEM(entry.shape, BF16),
                pltpu.SMEM(books.shape, jnp.int32),
                pltpu.VMEM(table.shape, BF16),
                pltpu.VMEM((ROWS, 2, ctx, kv_width), BF16),
                pltpu.VMEM((ROWS, HEADS * STEPS, kv_width), F32),
                pltpu.VMEM((T, D), F32),
                pltpu.VMEM((T, STAT), F32),
                pltpu.VMEM((lines, ctx), F32),
                pltpu.VMEM((lines, ctx), BF16),
                pltpu.SemaphoreType.DMA((6,)),
                pltpu.SemaphoreType.DMA((2, 2)),
                pltpu.SemaphoreType.DMA((1,)),
            ],
            places=(vmem(), vmem(), hbm()),
        )(*(in_hbm(v) for v in (held[0], *held[2:], cache, entry, books, table, weights[0])), entry_got, table_got)
        return experts(D, sent, *held[:2], held[3], gate, *weights[1:]), unused

    def waiting(entry, entry_got, books, table, table_got, cache, weights, *held):
        return jnp.zeros((T, D), BF16), traded(cache)

    def second(rows, cache, weights, *held):
        lines = ROWS * GROUPS * STEPS
        span = KV_HEADS * ctx
        share = GROUPS * HEAD_DIM
        sent, gate = call(
            attend_body,
            "attend",
            [hbm()] * 5 + [vmem()],
            (shape(width, share + STAT), shape(*gate_weight.shape[2:])),
            [
                *small(held[0], *held[2:]),
                pltpu.VMEM((ROWS, 2, span, HEAD_DIM), BF16),
                pltpu.VMEM((T, D), F32),
                pltpu.VMEM((T, D), F32),
                pltpu.VMEM((ROWS, GROUPS * STEPS, HEAD_DIM), F32),
                pltpu.VMEM((T, share), F32),
                pltpu.VMEM((T, STAT), F32),
                pltpu.VMEM((lines, span), F32),
                pltpu.VMEM((lines, span), BF16),
                pltpu.SemaphoreType.DMA((3,)),
                pltpu.SemaphoreType.DMA((2, KV_HEADS)),
                pltpu.SemaphoreType.DMA((1,)),
            ],
        )(*(in_hbm(v) for v in (held[0], *held[2:], cache, weights[0])), rows)
        return experts(share, sent, *held[:2], held[3], gate, *weights[1:])

    held = (expert_ids, gate_weights, cache_lengths, norm_gains)
    weights = (gate_weight, up_weight, down_weight)
    rows, cache = lax.cond(
        section == 0,
        first,
        waiting,
        entry_rows,
        swapped(entry_rows),
        codebook_ids,
        codec_table,
        swapped(codec_table),
        cache_entries,
        weights,
        *held,
    )
    rows = lax.cond(
        section == 1,
        second,
        lambda *values: jnp.zeros((T, D), BF16),
        swapped(rows),
        cache,
        weights,
        *held,
    )
    rows_got = swapped(rows)
    return call(
        head_body,
        "head",
        [vmem()] * 4,
        shape(STEPS, ROWS, codes, dtype=F32),
    )(rows, rows_got, final_gain.reshape(1, D), codec_table)


def solution(mesh):
    placed = (
        P("section", "expert", None),
        P("section", "expert", None, "seq", None),
        P(None, "expert"),
        P("section", None, None),
        P("section", None, "expert", None),
        P("section", None, "expert", None),
        P("section", ("expert", "seq"), None, None),
        P("section", ("expert", "seq"), None, None),
        P("section", ("expert", "seq"), None, None),
        P(None, "expert"),
        P(("section", "seq"), None),
        P(),
    )
    return jax.shard_map(
        per_device,
        mesh=mesh,
        in_specs=placed,
        out_specs=P(None, "expert", ("section", "seq")),
        check_vma=False,
    )
```

```python
import functools

import jax
import jax.numpy as jnp
from jax import lax
from jax.experimental import pallas as pl
from jax.experimental.pallas import tpu as pltpu
from jax.sharding import PartitionSpec as P

F32 = jnp.float32
BF16 = jnp.bfloat16
STEPS = 4
ROWS = 8
D = 2048
HEAD_DIM = 128
HEADS = D // HEAD_DIM
KV_HEADS = 4
GROUPS = HEADS // KV_HEADS
TOP = 8
CAP = 2
N_EXPERT = 4
N_SEQ = 16
DESTS = N_EXPERT * N_SEQ
SLOTS = STEPS * CAP
T = STEPS * ROWS
STAT = 128
PAY = D + STAT
CHUNKS = 3
EPS = 1e-6
LOWEST = -1e30


def vmem():
    return pl.BlockSpec(memory_space=pltpu.VMEM)


def hbm():
    return pl.BlockSpec(memory_space=pltpu.HBM)


def smem():
    return pl.BlockSpec(memory_space=pltpu.SMEM)


def call(body, name, ins, outs, scratch=(), limit=24, places=None):
    return pl.pallas_call(
        body,
        name=name,
        in_specs=ins,
        out_shape=outs,
        out_specs=places or jax.tree.map(lambda _: vmem(), outs),
        scratch_shapes=scratch,
        compiler_params=pltpu.CompilerParams(vmem_limit_bytes=limit << 20),
    )


def shape(*dims, dtype=BF16):
    return jax.ShapeDtypeStruct(dims, dtype)


def iota(dims, axis):
    return lax.broadcasted_iota(jnp.int32, dims, axis)


def dot(a, b, dims=((1,), (0,))):
    return lax.dot_general(a, b, (dims, ((), ())), preferred_element_type=F32)


def row_order():
    to, source = iota((T, T), 0), iota((T, T), 1)
    return (source == (to % STEPS) * ROWS + to // STEPS).astype(F32).astype(BF16)


def rms(value, gain):
    return value * lax.rsqrt(jnp.mean(value * value, axis=1, keepdims=True) + EPS) * gain


def named_slots(ids, gates=None):
    width = DESTS * SLOTS
    column = iota((T, width), 1)
    row = iota((T, width), 0)
    same_step = (row // ROWS) == (column // CAP) % STEPS
    below, above = iota((T, T), 0), iota((T, T), 1)
    earlier = ((below // ROWS == above // ROWS) & (above < below)).astype(F32).astype(BF16)
    ids = ids[0].reshape(T, TOP)
    named = jnp.zeros((T, width), F32)
    weight = jnp.zeros((T, width), F32)
    if gates is not None:
        gates = gates[0].reshape(T, TOP)
        shares = gates / jnp.sum(gates, axis=1, keepdims=True)
    for k in range(TOP):
        match = (ids[:, k : k + 1] == column // SLOTS) & same_step
        named = jnp.where(match, 1.0, named)
        if gates is not None:
            weight = jnp.where(match, shares[:, k : k + 1], weight)
    keep = dot(earlier, named.astype(BF16)) == (column % CAP).astype(F32)
    return jnp.where(keep, named if gates is None else weight, 0.0)


def slot_rows(ids):
    return dot(named_slots(ids).astype(BF16), row_order(), ((0,), (1,))).astype(BF16)


def mix_rows(ids, gates, mixing):
    share = named_slots(ids, gates)
    high = share.astype(BF16)
    low = (share - high.astype(F32)).astype(BF16)
    mixing[:T] = dot(row_order(), high).astype(BF16)
    mixing[T:] = dot(row_order(), low).astype(BF16)


def codec_part(section, seq, books, tables):
    codes = tables[0].shape[0]
    line = iota((T, codes), 0)
    wanted = jnp.zeros((T, codes), jnp.int32)
    for row_at in range(ROWS):
        for step in range(STEPS):
            wanted = jnp.where(line == row_at * STEPS + step, books[step, row_at], wanted)
    found = jnp.zeros((T, D), F32)
    for owner, table in zip((section, 1 - section), tables):
        start = (owner * N_SEQ + seq) * codes
        picked = (wanted - start == iota((T, codes), 1)).astype(F32).astype(BF16)
        found = found + dot(picked, table[...])
    return found


def lay_queries(hidden, gain, queries, values):
    normed = rms(hidden, gain)
    values[...] = hidden
    queries[...] = jnp.zeros_like(queries)
    for r in range(ROWS):
        for h in range(HEADS):
            k = h // GROUPS
            at = h * STEPS
            queries[r, at : at + STEPS, k * HEAD_DIM : (k + 1) * HEAD_DIM] = normed[
                r * STEPS : (r + 1) * STEPS, h * HEAD_DIM : (h + 1) * HEAD_DIM
            ]


def cache_copies(cache, kv, sems):
    half = ROWS // 2
    return [
        pltpu.make_async_copy(cache.at[0, r : r + half, i], kv.at[r : r + half, i], sems.at[r // half, i])
        for i in range(2)
        for r in range(0, ROWS, half)
    ]


def softened(scores, live):
    score = jnp.where(live, scores * HEAD_DIM ** (-0.5), LOWEST)
    highest = jnp.max(score, axis=1, keepdims=True)
    weight = jnp.where(live, jnp.exp(score - highest), 0.0)
    total = jnp.sum(weight, axis=1, keepdims=True)
    some = total > 0.0
    safe = jnp.where(some, total, 1.0)
    return weight.astype(BF16), jnp.where(some, highest + jnp.log(safe), LOWEST), 1.0 / safe


def attend_rows(seq, lengths, kv, copies, queries, values, stats, scores, weights):
    lines = GROUPS * STEPS
    size = HEADS * STEPS
    ctx = scores.shape[1]
    lane = iota((STEPS, STAT), 1)
    step_of = iota((size, ctx), 0) % STEPS
    position = seq * ctx + iota((size, ctx), 1)
    for copy in copies[:2]:
        copy.wait()
    for r in range(ROWS):
        scores[r * size : (r + 1) * size] = dot(queries[r].astype(BF16), kv[r, 0], ((1,), (1,)))
    scales = []
    for r in range(ROWS):
        limit = jnp.where(step_of == 0, lengths[0, r], 0)
        for step in range(1, STEPS):
            limit = jnp.where(step_of == step, lengths[step, r], limit)
        weight, log_sum, scale = softened(scores[r * size : (r + 1) * size], position < limit)
        weights[r * size : (r + 1) * size] = weight
        scales.append(scale)
        logs = jnp.broadcast_to(log_sum, (size, STAT))
        line_stats = jnp.zeros((STEPS, STAT), F32)
        for h in range(HEADS):
            line_stats = jnp.where(lane == h, logs[h * STEPS : (h + 1) * STEPS], line_stats)
        stats[r * STEPS : (r + 1) * STEPS, :] = line_stats
    for copy in copies[2:]:
        copy.wait()
    for r in range(ROWS):
        outs = dot(weights[r * size : (r + 1) * size], kv[r, 1])
        rows_at = slice(r * STEPS, (r + 1) * STEPS)
        for k in range(KV_HEADS):
            span = slice(k * lines, (k + 1) * lines)
            out = outs[span, k * HEAD_DIM : (k + 1) * HEAD_DIM] * scales[r][span]
            for g in range(GROUPS):
                h = k * GROUPS + g
                lanes_at = slice(h * HEAD_DIM, (h + 1) * HEAD_DIM)
                values[rows_at, lanes_at] = values[rows_at, lanes_at] + out[g * STEPS : (g + 1) * STEPS]


def spread_rows(values, stats, pick, sent):
    width = values.shape[1]
    heads = width // HEAD_DIM
    logs = stats[...]
    high = logs.astype(BF16).astype(F32)
    mid = (logs - high).astype(BF16).astype(F32)
    low = (logs - high - mid).astype(BF16).astype(F32)
    lane = iota((T, STAT), 1)
    packed = jnp.where(lane < 2 * heads, pltpu.roll(mid, heads, 1), pltpu.roll(low, 2 * heads, 1))
    packed = jnp.where(lane < heads, high, jnp.where(lane < 3 * heads, packed, 0.0))
    for at in range(0, width, 512):
        sent[:, at : at + 512] = dot(pick, values[:, at : at + 512].astype(BF16)).astype(BF16)
    sent[:, width : width + STAT] = dot(pick, packed.astype(BF16)).astype(BF16)


def enter_body(
    ids_in, lengths_in, gains_in, cache, entry_in, books_in, table_in, gate_in, entry_got, table_got,
    sent, gate, unused,
    ids, lengths, gains, entry, books, table, kv, queries, values, stats, scores, weights, small_sems, sems, ahead_sem,
):
    section = lax.axis_index("section")
    seq = lax.axis_index("seq")
    pairs = (
        (entry_in, entry),
        (gains_in, gains),
        (ids_in, ids),
        (lengths_in, lengths),
        (books_in, books),
        (table_in, table),
    )
    small = [pltpu.make_async_copy(source, target, small_sems.at[i]) for i, (source, target) in enumerate(pairs)]
    copies = cache_copies(cache, kv, sems)
    ahead = pltpu.make_async_copy(gate_in.at[0, 0], gate, ahead_sem.at[0])
    for copy in [*small, *copies, ahead]:
        copy.start()
    for copy in small:
        copy.wait()
    a = entry[...].astype(F32).reshape(T // 2, D)
    b = entry_got[...].astype(F32).reshape(T // 2, D)
    rows = jnp.where(section == 0, jnp.concatenate([a, b], axis=0), jnp.concatenate([b, a], axis=0))
    lay_queries(dot(row_order(), rows.astype(BF16)), gains[0, 0:1, :], queries, values)
    pick = slot_rows(ids)
    codes = codec_part(section, seq, books, (table, table_got))
    tiles = [
        codes[x * SLOTS : (x + 1) * SLOTS, s * STAT : (s + 1) * STAT] for x in range(N_EXPERT) for s in range(N_SEQ)
    ]
    sent[:, PAY:] = jnp.concatenate(tiles, axis=0).astype(BF16)
    attend_rows(seq, lengths, kv, copies, queries, values, stats, scores, weights)
    spread_rows(values, stats, pick, sent)
    ahead.wait()


def trade_body(cache, out, held, parts, in_sems, out_sems):
    copies = [pltpu.make_async_copy(cache.at[0, r], held.at[r], in_sems.at[r]) for r in range(ROWS)]
    for copy in copies:
        copy.start()
    sends = []
    for r in range(ROWS):
        copies[r].wait()
        for k in range(KV_HEADS):
            parts[k, r] = held[r, :, :, k * HEAD_DIM : (k + 1) * HEAD_DIM]
    for k in range(KV_HEADS):
        sends.append(pltpu.make_async_copy(parts.at[k], out.at[k], out_sems.at[k]))
        sends[-1].start()
    for send in sends:
        send.wait()


def attend_body(
    ids_in, lengths_in, gains_in, cache, gate_in, rows,
    sent, gate,
    ids, lengths, gains, kv, normed, hidden, queries, values, stats, scores, weights, small_sems, sems, ahead_sem,
):
    seq = lax.axis_index("seq")
    pairs = ((gains_in, gains), (ids_in, ids), (lengths_in, lengths))
    small = [pltpu.make_async_copy(source, target, small_sems.at[i]) for i, (source, target) in enumerate(pairs)]
    local = cache.shape[3]
    copies = [
        pltpu.make_async_copy(cache.at[y, :, i], kv.at[:, i, y * local : (y + 1) * local], sems.at[i, y])
        for i in range(2)
        for y in range(KV_HEADS)
    ]
    ahead = pltpu.make_async_copy(gate_in.at[0, 0], gate, ahead_sem.at[0])
    for copy in [*small, *copies, ahead]:
        copy.start()
    whole = rows[...].astype(F32)
    hidden[...] = whole
    for copy in small:
        copy.wait()
    normed[...] = rms(whole, gains[0, 0:1, :])
    width = values.shape[1]
    own = pl.ds(pl.multiple_of((seq % KV_HEADS) * width, width), width)
    asked = normed[:, own]
    values[...] = hidden[:, own]
    size = GROUPS * STEPS
    for r in range(ROWS):
        for g in range(GROUPS):
            queries[r, g * STEPS : (g + 1) * STEPS, :] = asked[
                r * STEPS : (r + 1) * STEPS, g * HEAD_DIM : (g + 1) * HEAD_DIM
            ]
    pick = slot_rows(ids)
    for copy in copies[:KV_HEADS]:
        copy.wait()
    for r in range(ROWS):
        scores[r * size : (r + 1) * size] = dot(queries[r].astype(BF16), kv[r, 0], ((1,), (1,)))
    ctx = scores.shape[1]
    step_of = iota((size, ctx), 0) % STEPS
    position = (seq // KV_HEADS) * ctx + iota((size, ctx), 1)
    lane = iota((STEPS, STAT), 1)
    scales = []
    for r in range(ROWS):
        limit = jnp.where(step_of == 0, lengths[0, r], 0)
        for step in range(1, STEPS):
            limit = jnp.where(step_of == step, lengths[step, r], limit)
        weight, log_sum, scale = softened(scores[r * size : (r + 1) * size], position < limit)
        weights[r * size : (r + 1) * size] = weight
        scales.append(scale)
        logs = jnp.broadcast_to(log_sum, (size, STAT))
        line_stats = jnp.zeros((STEPS, STAT), F32)
        for g in range(GROUPS):
            line_stats = jnp.where(lane == g, logs[g * STEPS : (g + 1) * STEPS], line_stats)
        stats[r * STEPS : (r + 1) * STEPS, :] = line_stats
    for copy in copies[KV_HEADS:]:
        copy.wait()
    for r in range(ROWS):
        out = dot(weights[r * size : (r + 1) * size], kv[r, 1]) * scales[r]
        rows_at = slice(r * STEPS, (r + 1) * STEPS)
        for g in range(GROUPS):
            lanes_at = slice(g * HEAD_DIM, (g + 1) * HEAD_DIM)
            values[rows_at, lanes_at] = values[rows_at, lanes_at] + out[g * STEPS : (g + 1) * STEPS]
    spread_rows(values, stats, pick, sent)
    ahead.wait()


def expert_body(
    width, got, ids_in, gates_in, gains_in, gate, up_in, down_in,
    sent, mixing,
    middle, ids, gates, gains, up, down, sems,
):
    block = N_SEQ * SLOTS
    size = gate.shape[0] // CHUNKS
    pairs = [(gains_in, gains), (ids_in, ids), (gates_in, gates)]
    for source, target in ((up_in, up), (down_in, down)):
        for j in range(0, CHUNKS * size, size):
            pairs.append((source.at[0, 0, j : j + size], target.at[j : j + size]))
    copies = [pltpu.make_async_copy(source, target, sems.at[i]) for i, (source, target) in enumerate(pairs)]
    for copy in copies:
        copy.start()
    heads = width // HEAD_DIM
    widen = (iota((2 * STAT, width), 0) % STAT == iota((2 * STAT, width), 1) // HEAD_DIM).astype(F32).astype(BF16)
    parts = D // width
    lines = parts * SLOTS
    for x in range(N_EXPERT):
        rows_at = slice(x * block, (x + 1) * block)
        packed = got[rows_at, width : width + STAT].astype(F32)
        logs = packed + pltpu.roll(packed, STAT - heads, 1) + pltpu.roll(packed, STAT - 2 * heads, 1)
        logs = logs.reshape(block // lines, lines, STAT)
        weights = jnp.exp(logs - jnp.max(logs, axis=0, keepdims=True))
        weights = weights / jnp.sum(weights, axis=0, keepdims=True)
        weights = weights.reshape(block, STAT)
        high = weights.astype(BF16)
        low = (weights - high.astype(F32)).astype(BF16)
        weights = jnp.concatenate([high, low], axis=1)
        for at in range(0, width, 256):
            lanes_at = slice(at, at + 256)
            wide = dot(weights, widen[:, lanes_at])
            part = (got[rows_at, lanes_at].astype(F32) * wide).reshape(block // lines, lines, 256)
            part = jnp.sum(part, axis=0)
            for y in range(parts):
                middle[x * SLOTS : (x + 1) * SLOTS, y * width + at : y * width + at + 256] = part[
                    y * SLOTS : (y + 1) * SLOTS
                ]
    rows = middle[...]
    for copy in copies[:3]:
        copy.wait()
    moe_in = rms(rows, gains[0, 1:2, :]).astype(BF16)
    activ = []
    for j in range(CHUNKS):
        at = slice(j * size, (j + 1) * size)
        copies[3 + j].wait()
        gate_out = dot(moe_in, gate[at], ((1,), (1,)))
        up_out = dot(moe_in, up[at], ((1,), (1,)))
        activ.append((gate_out / (1.0 + jnp.exp(-gate_out)) * up_out).astype(BF16))
    mix_rows(ids, gates, mixing)
    total = jnp.zeros((T, D), F32)
    for j in range(CHUNKS):
        copies[3 + CHUNKS + j].wait()
        total = total + dot(activ[j], down[j * size : (j + 1) * size])
    result = total.astype(BF16).astype(F32) + rows
    coded = got.shape[1] > width + STAT
    if coded:
        codes = jnp.sum(got[:, width + STAT :].astype(F32).reshape(N_EXPERT, N_SEQ, SLOTS, STAT), axis=1)
    for x in range(N_EXPERT):
        part = result[x * SLOTS : (x + 1) * SLOTS]
        if coded:
            part = jnp.concatenate([part, codes[x]], axis=1)
        pair = jnp.concatenate([part, part], axis=0).astype(BF16)
        for s in range(0, N_SEQ, 2):
            at = (x * N_SEQ + s) * SLOTS
            sent[at : at + 2 * SLOTS, :] = pair


def mix_body(got, mixing, out):
    both = dot(mixing[...], got[:, :D])
    hidden = (both[:T] + both[T:]).astype(BF16)
    if got.shape[1] > D:
        codes = got[:, D:].astype(F32)
        lines = [
            jnp.concatenate(
                [codes[(x * N_SEQ + s) * SLOTS : (x * N_SEQ + s + 1) * SLOTS] for s in range(N_SEQ)], axis=1
            )
            for x in range(N_EXPERT)
        ]
        hidden = hidden.astype(F32) + jnp.concatenate(lines, axis=0)
    out[...] = hidden.astype(out.dtype)


def head_body(mine, got, gain, table, out):
    last = lax.axis_index("section") == 1
    hidden = jnp.where(last, mine[...].astype(F32), got[...].astype(F32))
    final = rms(hidden, gain[...]).astype(BF16)
    final = dot(row_order(), final, ((0,), (0,))).astype(BF16)
    logits = dot(final, table[...], ((1,), (1,))) * D ** (-0.5)
    out[...] = logits.reshape(out.shape)


def in_hbm(value):
    return pltpu.with_memory_space_constraint(value, pltpu.HBM)


def swapped(value):
    return lax.ppermute(value, "section", [(0, 1), (1, 0)])


def exchanged(value):
    return lax.all_to_all(value, ("expert", "seq"), 0, 0, tiled=True)


def traded(cache):
    _, rows, kinds, ctx, _ = cache.shape
    parts = pl.pallas_call(
        trade_body,
        name="trade",
        in_specs=[hbm()],
        out_specs=hbm(),
        out_shape=shape(KV_HEADS, rows, kinds, ctx, HEAD_DIM),
        scratch_shapes=[
            pltpu.VMEM(cache.shape[1:], BF16),
            pltpu.VMEM((KV_HEADS, rows, kinds, ctx, HEAD_DIM), BF16),
            pltpu.SemaphoreType.DMA((rows,)),
            pltpu.SemaphoreType.DMA((KV_HEADS,)),
        ],
        compiler_params=pltpu.CompilerParams(vmem_limit_bytes=56 << 20),
    )(in_hbm(cache))
    groups = [list(range(at, at + KV_HEADS)) for at in range(0, N_SEQ, KV_HEADS)]
    return lax.all_to_all(parts, "seq", 0, 0, axis_index_groups=groups, tiled=True)


def experts(width, sent, ids, gates, gains, gate, up, down):
    coded = STAT if sent.shape[1] > width + STAT else 0
    sent, mixing = call(
        functools.partial(expert_body, width),
        "experts",
        [vmem()] + [hbm()] * 3 + [vmem()] + [hbm()] * 2,
        (shape(DESTS * SLOTS, D + coded), shape(2 * T, DESTS * SLOTS)),
        [
            pltpu.VMEM((T, D), F32),
            pltpu.VMEM(ids.shape, jnp.int32),
            pltpu.VMEM(gates.shape, F32),
            pltpu.VMEM(gains.shape, F32),
            *(pltpu.VMEM(weight.shape[2:], BF16) for weight in (up, down)),
            pltpu.SemaphoreType.DMA((3 + 2 * CHUNKS,)),
        ],
    )(exchanged(sent), in_hbm(ids), in_hbm(gates), in_hbm(gains), gate, in_hbm(up), in_hbm(down))
    return call(mix_body, "mix", [vmem()] * 2, shape(T, D))(exchanged(sent), mixing)


def per_device(
    entry_rows,
    cache_entries,
    cache_lengths,
    norm_gains,
    expert_ids,
    gate_weights,
    gate_weight,
    up_weight,
    down_weight,
    codebook_ids,
    codec_table,
    final_gain,
):
    codes = codec_table.shape[0]
    section = lax.axis_index("section")
    ctx = cache_entries.shape[3]
    kv_width = cache_entries.shape[4]
    width = DESTS * SLOTS

    def small(ids, lengths, gains):
        return [
            pltpu.VMEM(ids.shape, jnp.int32),
            pltpu.SMEM(lengths.shape, jnp.int32),
            pltpu.VMEM(gains.shape, F32),
        ]

    def first(entry, entry_got, books, table, table_got, cache, weights, *held):
        lines = ROWS * HEADS * STEPS
        sent, gate, unused = call(
            enter_body,
            "enter",
            [hbm()] * 8 + [vmem()] * 2,
            (shape(width, PAY + STAT), shape(*gate_weight.shape[2:]), shape(KV_HEADS, ROWS, 2, ctx, HEAD_DIM)),
            [
                *small(held[0], *held[2:]),
                pltpu.VMEM(entry.shape, BF16),
                pltpu.SMEM(books.shape, jnp.int32),
                pltpu.VMEM(table.shape, BF16),
                pltpu.VMEM((ROWS, 2, ctx, kv_width), BF16),
                pltpu.VMEM((ROWS, HEADS * STEPS, kv_width), F32),
                pltpu.VMEM((T, D), F32),
                pltpu.VMEM((T, STAT), F32),
                pltpu.VMEM((lines, ctx), F32),
                pltpu.VMEM((lines, ctx), BF16),
                pltpu.SemaphoreType.DMA((6,)),
                pltpu.SemaphoreType.DMA((2, 2)),
                pltpu.SemaphoreType.DMA((1,)),
            ],
            places=(vmem(), vmem(), hbm()),
        )(*(in_hbm(v) for v in (held[0], *held[2:], cache, entry, books, table, weights[0])), entry_got, table_got)
        return experts(D, sent, *held[:2], held[3], gate, *weights[1:]), unused

    def waiting(entry, entry_got, books, table, table_got, cache, weights, *held):
        return jnp.zeros((T, D), BF16), traded(cache)

    def second(rows, cache, weights, *held):
        lines = ROWS * GROUPS * STEPS
        span = KV_HEADS * ctx
        share = GROUPS * HEAD_DIM
        sent, gate = call(
            attend_body,
            "attend",
            [hbm()] * 5 + [vmem()],
            (shape(width, share + STAT), shape(*gate_weight.shape[2:])),
            [
                *small(held[0], *held[2:]),
                pltpu.VMEM((ROWS, 2, span, HEAD_DIM), BF16),
                pltpu.VMEM((T, D), F32),
                pltpu.VMEM((T, D), F32),
                pltpu.VMEM((ROWS, GROUPS * STEPS, HEAD_DIM), F32),
                pltpu.VMEM((T, share), F32),
                pltpu.VMEM((T, STAT), F32),
                pltpu.VMEM((lines, span), F32),
                pltpu.VMEM((lines, span), BF16),
                pltpu.SemaphoreType.DMA((3,)),
                pltpu.SemaphoreType.DMA((2, KV_HEADS)),
                pltpu.SemaphoreType.DMA((1,)),
            ],
        )(*(in_hbm(v) for v in (held[0], *held[2:], cache, weights[0])), rows)
        return experts(share, sent, *held[:2], held[3], gate, *weights[1:])

    held = (expert_ids, gate_weights, cache_lengths, norm_gains)
    weights = (gate_weight, up_weight, down_weight)
    rows, cache = lax.cond(
        section == 0,
        first,
        waiting,
        entry_rows,
        swapped(entry_rows),
        codebook_ids,
        codec_table,
        swapped(codec_table),
        cache_entries,
        weights,
        *held,
    )
    rows = lax.cond(
        section == 1,
        second,
        lambda *values: jnp.zeros((T, D), BF16),
        swapped(rows),
        cache,
        weights,
        *held,
    )
    rows_got = swapped(rows)
    return call(
        head_body,
        "head",
        [vmem()] * 4,
        shape(STEPS, ROWS, codes, dtype=F32),
    )(rows, rows_got, final_gain.reshape(1, D), codec_table)


def solution(mesh):
    placed = (
        P("section", "expert", None),
        P("section", "expert", None, "seq", None),
        P(None, "expert"),
        P("section", None, None),
        P("section", None, "expert", None),
        P("section", None, "expert", None),
        P("section", ("expert", "seq"), None, None),
        P("section", ("expert", "seq"), None, None),
        P("section", ("expert", "seq"), None, None),
        P(None, "expert"),
        P(("section", "seq"), None),
        P(),
    )
    return jax.shard_map(
        per_device,
        mesh=mesh,
        in_specs=placed,
        out_specs=P(None, "expert", ("section", "seq")),
        check_vma=False,
    )
```
